128 devices in a mesh: tower: 2 (over core), seq: 32 (over z_lo, y, x), mp: 2 (over z_hi).
Axes of the slice: x: 4, y: 4, z: 4 (z_hi: 2, z_lo: 2; z = z_hi * 2 + z_lo), core: 2. Of those that a mesh axis runs over, the one named last changes fastest.
Arguments:
- queries: bfloat16 [2, 8192, 1536], P('tower', 'seq', 'mp'), as said below
- context: bfloat16 [2, 8192, 3072], P('tower', 'seq'), may hold values from -6 to 6
- kv_weight: bfloat16 [2, 3072, 2, 1536], P('tower', None, None, 'mp'), may hold values from -0.109375 to 0.109375
- spans: int32 [2, 32, 2], P('tower', 'seq'), may hold values from 0 to 31, as said below
- cotangent: bfloat16 [2, 8192, 1536], P('tower', 'seq', 'mp'), may hold values from -6 to 6
Outputs:
- attn_out: bfloat16 [2, 8192, 1536], P('tower', 'seq', 'mp')
- query_grad: bfloat16 [2, 8192, 1536], P('tower', 'seq', 'mp')
- context_grad: bfloat16 [2, 8192, 3072], P('tower', 'seq')
- weight_grad: bfloat16 [2, 3072, 2, 1536], P('tower', 'seq', None, 'mp')
The draws below stay inside these ranges and needn't reach their ends.
Inputs may be any that keep to these rules, and one draw needn't show every extreme that they name: queries are drawn independently per entry; their rows may differ in scale. For shard s, s - 2 <= spans[t, s, 0] <= s <= spans[t, s, 1] <= s + 2; in each tower some shard has spans[t, s, 1] - spans[t, s, 0] = 4.
All inputs are finite; a program needn't handle non-finite values.
Results may differ from the reference program's by a relative error of at most 0.03.
Values may be sent and summed in bfloat16 or wider, within the bound.
No kernel may reach another device: no remote copies, remote signals or barrier semaphores. Data moves between devices by JAX's collectives and lax.ppermute only.
A program may use at most 128 MiB of HBM per device.

```python
import jax
import jax.numpy as jnp
from jax import lax

D = 3072
HD = 128
HEADS = 12
TOK_DEV = 256
REACH = 2
TOKENS = 8192
N_SEQ = 32


def draw_queries(key, part):
    key = jax.random.fold_in(key, 11)
    base = jax.random.normal(key, (2, TOKENS, HEADS * HD), jnp.float32)
    base = jnp.clip(base, -6.0, 6.0)
    return base.astype(jnp.bfloat16)


def draw_spans(key, part):
    key = jax.random.fold_in(key, 21)
    below = jax.random.randint(jax.random.fold_in(key, 1), (2, N_SEQ), 0, REACH + 1)
    above = jax.random.randint(jax.random.fold_in(key, 2), (2, N_SEQ), 0, REACH + 1)
    shard = jnp.arange(N_SEQ, dtype=jnp.int32)[None, :]
    middle = N_SEQ // 2
    below = jnp.where(shard == middle, REACH, below)
    above = jnp.where(shard == middle, REACH, above)
    span_low = jnp.maximum(shard - below, 0)
    span_high = jnp.minimum(shard + above, N_SEQ - 1)
    return jnp.stack([span_low, span_high], axis=2).astype(jnp.int32)


def with_spikes(values, stream_key, source, target, parts, factor):
    owner, partner = [(jnp.arange(values.shape[dim]) // (values.shape[dim] // parts)).reshape([-1 if axis == dim else 1 for axis in range(values.ndim)]) for dim in (source, target)]
    chosen = jax.random.permutation(stream_key, parts)[partner]
    strong = (owner == chosen) | (owner == (partner + parts // 2) % parts)
    return jnp.where(strong, factor * values, values)


def block_levels(rng, shape, cuts, smallest, high):
    level, own = 1.0, jax.random.fold_in(rng, 6)
    for dim, shards_of in cuts:
        heights = jnp.exp(jax.random.uniform(jax.random.fold_in(own, dim), (shards_of,), jnp.float32, smallest / len(cuts), high / len(cuts)))
        level = level * jnp.repeat(heights, shape[dim] // shards_of).reshape([-1 if axis == dim else 1 for axis in range(len(shape))])
    return level


def bell_draw(rng, dims, scale, bound, shards=(), kind=jnp.bfloat16):
    values = scale * jax.random.normal(rng, dims, jnp.float32)
    if shards:
        values = values * block_levels(rng, dims, shards, -0.22, 0.18)
    return jnp.clip(values, -bound, bound).astype(kind)


def heavy_noise(rng, dims, spread, limit, shards, heavy, held_as=jnp.bfloat16):
    values = spread * jax.random.normal(rng, dims, jnp.float32)
    if shards:
        values = values * block_levels(rng, dims, shards, -0.22, 0.18)
    return jnp.clip(with_spikes(values, jax.random.fold_in(rng, 3), *heavy), -limit, limit).astype(held_as)


def setup_inputs(seed: int = 0) -> dict:
    key_list = jax.random.split(jax.random.key(seed), 6)
    queries = draw_queries(jax.random.fold_in(key_list[5], 71), 0)
    context = heavy_noise(key_list[1], (2, TOKENS, D), 1.0, 6.0, ((0, 2), (1, 32)), (1, 2, 32, 2.75))
    kv_weight = bell_draw(key_list[2], (2, D, 2, HEADS * HD), D ** -0.5, 0.109375, ((0, 2), (3, 2)))
    spans = draw_spans(jax.random.fold_in(key_list[5], 71), 0)
    cotangent = bell_draw(key_list[4], (2, TOKENS, HEADS * HD), 1.0, 6.0, ((0, 2), (1, 32), (2, 2)))
    return {"queries": queries, "context": context, "kv_weight": kv_weight, "spans": spans, "cotangent": cotangent}


NEG_FILL = -1e30


def shard_partials(left, right):
    left_blocks = left.reshape(N_SEQ, TOK_DEV, -1).astype(jnp.float32)
    right_blocks = right.reshape(N_SEQ, TOK_DEV, -1).astype(jnp.float32)
    partial_value = jnp.einsum("sik,sid->skd", left_blocks, right_blocks)
    partial_value = lax.optimization_barrier(partial_value.astype(jnp.bfloat16))
    return jnp.sum(partial_value.astype(jnp.float32), axis=0)


def attend_head(q_head, k_head, v_head, cot_head, allowed):
    scale = HD ** -0.5
    scores = jnp.dot(q_head, k_head.T, preferred_element_type=jnp.float32) * scale
    scores = jnp.where(allowed, scores, NEG_FILL)
    row_max = jnp.max(scores, axis=1, keepdims=True)
    expo = jnp.where(allowed, jnp.exp(scores - row_max), 0.0)
    weights = expo / jnp.sum(expo, axis=1, keepdims=True)
    rounded = weights.astype(jnp.bfloat16)
    output = jnp.dot(rounded, v_head, preferred_element_type=jnp.float32).astype(jnp.bfloat16)
    dprob = jnp.dot(cot_head, v_head.T, preferred_element_type=jnp.float32)
    delta = jnp.sum(dprob * weights, axis=1, keepdims=True)
    dscore = (weights * (dprob - delta) * scale).astype(jnp.bfloat16)
    q_grad = jnp.dot(dscore, k_head, preferred_element_type=jnp.float32).astype(jnp.bfloat16)
    key_part = shard_partials(dscore, q_head)
    value_part = shard_partials(rounded, cot_head)
    return output, q_grad, key_part, value_part


def heads_first(array):
    return array.reshape(TOKENS, HEADS, HD).transpose(1, 0, 2)


def heads_back(array):
    return array.transpose(1, 0, 2).reshape(TOKENS, HEADS * HD)


def reference(queries, context, kv_weight, spans, cotangent):
    columns = HEADS * HD
    flat_weights = [kv_weight[side].reshape(D, 2 * columns) for side in range(2)]
    key_values = [jnp.dot(context[side], flat_weights[side], preferred_element_type=jnp.float32).astype(jnp.bfloat16) for side in range(2)]
    shard_rows = jnp.arange(TOKENS, dtype=jnp.int32) // TOK_DEV
    outputs = [None, None]
    q_grads = [None, None]
    kv_grads = [None, None]
    for side in range(2):
        source = 1 - side
        span_low = spans[side, :, 0][shard_rows]
        span_high = spans[side, :, 1][shard_rows]
        allowed = (shard_rows[None, :] >= span_low[:, None]) & (shard_rows[None, :] <= span_high[:, None])

        def per_head(operands):
            q_head, k_head, v_head, cot_head = operands
            return attend_head(q_head, k_head, v_head, cot_head, allowed)

        stacked = (heads_first(queries[side]), heads_first(key_values[source][:, :columns]),
                   heads_first(key_values[source][:, columns:]), heads_first(cotangent[side]))
        output, q_grad, key_part, value_part = lax.map(per_head, stacked)
        outputs[side] = heads_back(output)
        q_grads[side] = heads_back(q_grad)
        kv_grads[source] = jnp.concatenate([heads_back(key_part), heads_back(value_part)], axis=1).astype(jnp.bfloat16)
    context_grads = []
    weight_grads = []
    for side in range(2):
        context_grads.append(jnp.dot(kv_grads[side], flat_weights[side].T, preferred_element_type=jnp.float32).astype(jnp.bfloat16))

        def add_shard(total, pair):
            ctx_block, grad_block = pair
            partial_value = jnp.dot(ctx_block.T, grad_block, preferred_element_type=jnp.float32)
            partial_value = lax.optimization_barrier(partial_value.astype(jnp.bfloat16))
            return total + partial_value.astype(jnp.float32), None

        total, unused = lax.scan(add_shard, jnp.zeros((D, 2 * columns), jnp.float32),
                                 (context[side].reshape(N_SEQ, TOK_DEV, D), kv_grads[side].reshape(N_SEQ, TOK_DEV, 2 * columns)))
        weight_grads.append(total.astype(jnp.bfloat16).reshape(D, 2, columns))
    return (jnp.stack(outputs), jnp.stack(q_grads), jnp.stack(context_grads), jnp.stack(weight_grads))
```

```python
import functools

import jax
import jax.numpy as jnp
from jax import lax
from jax.experimental import pallas as pl
from jax.experimental.pallas import tpu as pltpu
from jax.sharding import PartitionSpec as P

HD = 128
REACH = 2
NEG_FILL = -1e30
F32, BF16 = jnp.float32, jnp.bfloat16
ZS, YS, XS = 2, 4, 4
PAIR = 2
WINDOW = 6


def moved(value, axis, pairs):
    return lax.ppermute(value, axis, pairs)


def swapped(value, axis):
    return moved(value, axis, [(0, 1), (1, 0)])


def seq_pairs(to):
    pairs = []
    for source in range(ZS * YS * XS):
        target = to(source // (YS * XS), source // XS % YS, source % XS)
        if target is not None:
            z, y, x = target
            pairs.append((source, (z * YS + y % YS) * XS + x % XS))
    return pairs


def along_x(steps):
    return seq_pairs(lambda z, y, x: (z, y, x + steps))


def along_y(steps):
    return seq_pairs(lambda z, y, x: (z, y + steps, x))


def across_z():
    return seq_pairs(lambda z, y, x: (1 - z, y, x))


def to_pair(steps, same):
    count = ZS * YS * XS
    pairs = []
    for source in range(count):
        pair, member = source // PAIR, source % PAIR
        target = (pair + steps) * PAIR + (member if same else 1 - member)
        if 0 <= target < count:
            pairs.append((source, target))
    return pairs


def dot(a, b, dims):
    return lax.dot_general(a, b, ((dims[0], dims[1]), ((), ())), preferred_element_type=F32)


def attention_kernel(meta, q_own, c_own, q_pair, c_pair, *refs):
    kv_refs, (od_own, od_pair), g_refs = refs[:6], refs[6:8], refs[8:14]
    kv_s, q_s, c_s, g_s = refs[14:]
    rows = q_own.shape[0]
    member = meta[0]
    scale = HD ** (-0.5)
    order = (2 + member, 3 - member, member, 1 - member, 4 + member, 5 - member)
    for ref, place in zip(kv_refs, order):
        kv_s[pl.ds(pl.multiple_of(place * rows, rows), rows), :] = ref[...]
    for ref, pair_ref, scratch in ((q_own, q_pair, q_s), (c_own, c_pair, c_s)):
        scratch[pl.ds(pl.multiple_of(member * rows, rows), rows), :] = ref[...]
        scratch[pl.ds(pl.multiple_of((1 - member) * rows, rows), rows), :] = pair_ref[...]
    g_s[...] = jnp.zeros_like(g_s)
    span = 2 * REACH + 1
    for i in range(PAIR):
        q = q_s[i * rows : (i + 1) * rows, :]
        c = c_s[i * rows : (i + 1) * rows, :]
        window = slice(i * rows, (i + span) * rows)
        keys = kv_s[window, :HD]
        values = kv_s[window, HD:]
        low, high = meta[2 + 2 * i], meta[3 + 2 * i]
        scores = dot(keys, q, ((1,), (1,))) * scale
        blocks = []
        for j in range(span):
            shard = meta[1] + i + j
            keep = (shard >= low) & (shard <= high)
            blocks.append(jnp.where(keep, scores[j * rows : (j + 1) * rows], NEG_FILL))
        scores = jnp.concatenate(blocks, axis=0)
        expo = jnp.exp(scores - jnp.max(scores, axis=0, keepdims=True))
        probs = expo * (1.0 / jnp.sum(expo, axis=0, keepdims=True))
        rounded = probs.astype(BF16)
        dprobs = dot(values, c, ((1,), (1,)))
        delta = jnp.sum(dprobs * probs, axis=0, keepdims=True)
        dscores = (probs * (dprobs - delta) * scale).astype(BF16)
        out = dot(values, rounded, ((0,), (0,)))
        dq = dot(keys, dscores, ((0,), (0,)))
        g_s[window, :HD] += dot(dscores, q, ((1,), (0,)))
        g_s[window, HD:] += dot(rounded, c, ((1,), (0,)))
        both = jnp.concatenate([out, dq], axis=0).T.astype(BF16)

        @pl.when(member == i)
        def _():
            od_own[...] = both

        @pl.when(member != i)
        def _():
            od_pair[...] = both

    for ref, place in zip(g_refs, order):
        ref[...] = g_s[pl.ds(pl.multiple_of(place * rows, rows), rows), :].astype(BF16)


def attention(meta, queries, cotangent, arrived_qc, kv_own, kv_rest):
    rows, columns = queries.shape
    heads = columns // HD // PAIR
    half = heads * 2 * HD
    one = lambda of: pl.BlockSpec((rows, HD), of)
    two = lambda of: pl.BlockSpec((rows, 2 * HD), of)
    plain = two(lambda h, m: (0, h))
    own = lambda h, m: (0, heads * m[0] + h)
    shape = jax.ShapeDtypeStruct((rows, half), BF16)
    work = 2 * heads * rows * rows * 5
    return pl.pallas_call(
        attention_kernel,
        out_shape=[shape] * 8,
        grid_spec=pltpu.PrefetchScalarGridSpec(
            num_scalar_prefetch=1,
            grid=(heads,),
            in_specs=[
                one(own),
                one(own),
                one(lambda h, m: (0, h)),
                one(lambda h, m: (0, heads + h)),
                two(own),
            ]
            + [plain] * 5,
            out_specs=[plain] * 8,
            scratch_shapes=[
                pltpu.VMEM((WINDOW * rows, 2 * HD), BF16),
                pltpu.VMEM((PAIR * rows, HD), BF16),
                pltpu.VMEM((PAIR * rows, HD), BF16),
                pltpu.VMEM((WINDOW * rows, 2 * HD), F32),
            ],
        ),
        compiler_params=pltpu.CompilerParams(vmem_limit_bytes=40 * 2**20),
        cost_estimate=pl.CostEstimate(
            flops=work * 10 * HD, bytes_accessed=8 * 2**20, transcendentals=work
        ),
        name="attention",
    )(meta, queries, cotangent, arrived_qc, arrived_qc, kv_own, *kv_rest)


def local(queries, context, kv_weight, spans, cotangent):
    queries, context, cotangent = queries[0], context[0], cotangent[0]
    rows, columns = queries.shape
    heads = columns // HD
    width = context.shape[1]
    half = columns
    position = lax.axis_index("seq")
    member = position % PAIR
    x, y, z = position % XS, position // XS % YS, position // (XS * YS)

    other_half = (1 - member) * (columns // 2)
    qc = jnp.concatenate(
        [lax.dynamic_slice_in_dim(v, other_half, columns // 2, axis=1) for v in (queries, cotangent)],
        axis=1,
    )
    pair_swap = to_pair(0, False)
    arrived_qc = moved(qc, "seq", pair_swap)
    own_span = spans[0, 0]
    pair_span = moved(own_span, "seq", pair_swap)

    by_y = context.reshape(rows, ZS, YS, width // (ZS * YS))
    ctx_part = lambda k: lax.dynamic_index_in_dim(by_y, (y + k) % YS, 2, keepdims=False).reshape(
        rows, width // YS
    )
    ctx_cols = [ctx_part(0)] + [moved(ctx_part(k), "seq", along_y(k)) for k in range(1, YS)]

    weight = (
        kv_weight[0].reshape(width, 2, heads, HD).transpose(0, 2, 1, 3).reshape(width, 2 * columns)
    )
    local_kv = dot(context, weight, ((1,), (0,))).astype(BF16)
    other_kv = swapped(local_kv, "tower")
    same_half = lax.dynamic_slice_in_dim(other_kv, member * half, half, axis=1)
    next_half = lax.dynamic_slice_in_dim(other_kv, (1 - member) * half, half, axis=1)
    kv_rest = [
        moved(next_half, "seq", pair_swap),
        moved(same_half, "seq", to_pair(1, True)),
        moved(next_half, "seq", to_pair(1, False)),
        moved(same_half, "seq", to_pair(-1, True)),
        moved(next_half, "seq", to_pair(-1, False)),
    ]
    first = jnp.where(member == 0, own_span, pair_span)
    second = jnp.where(member == 0, pair_span, own_span)
    base = position - member - REACH
    meta = jnp.concatenate([jnp.stack([member, base]), first, second]).astype(jnp.int32)
    od_own, od_pair, g_own, *g_rest = attention(
        meta, queries, cotangent, arrived_qc, other_kv, kv_rest
    )
    arrived = [
        moved(g, "seq", pairs)
        for g, pairs in zip(
            g_rest,
            (pair_swap, to_pair(-1, True), to_pair(-1, False), to_pair(1, True), to_pair(1, False)),
        )
    ]
    total = lambda parts: functools.reduce(jnp.add, [p.astype(F32) for p in parts]).astype(BF16)
    g_same = total([g_own, arrived[1], arrived[3]])
    g_next = total([arrived[0], arrived[2], arrived[4]])
    kv_grad = jnp.concatenate(
        [jnp.where(member == 0, g_same, g_next), jnp.where(member == 0, g_next, g_same)], axis=1
    )
    returned = swapped(kv_grad, "tower")

    gathered = [returned] + [moved(returned, "seq", along_y(k)) for k in range(1, YS)]

    partial_ctx = dot(returned, weight, ((1,), (1,))).astype(BF16)
    partial_ctx = lax.optimization_barrier(partial_ctx)
    context_grad = (
        partial_ctx.astype(F32) + swapped(partial_ctx, "mp").astype(F32)
    ).astype(BF16)

    partial_w = dot(
        jnp.concatenate(ctx_cols, axis=0), jnp.concatenate(gathered, axis=0), ((0,), (0,))
    ).astype(BF16)
    by_x = partial_w.reshape(ZS, XS, width // (ZS * YS * XS), 2 * columns)
    x_part = lambda k: lax.dynamic_index_in_dim(by_x, (x + k) % XS, 1, keepdims=False)
    over_x = functools.reduce(
        jnp.add,
        [x_part(0).astype(F32)]
        + [moved(x_part(k), "seq", along_x(k)).astype(F32) for k in range(1, XS)],
    )
    z_part = lambda k: lax.dynamic_index_in_dim(over_x, (z + k) % ZS, 0, keepdims=False)
    weight_grad = z_part(0) + moved(z_part(1).astype(BF16), "seq", across_z()).astype(F32)
    weight_grad = (
        weight_grad.astype(BF16)
        .reshape(-1, heads, 2, HD)
        .transpose(0, 2, 1, 3)
        .reshape(1, -1, 2, columns)
    )

    od_back = moved(od_pair, "seq", pair_swap)
    lo = jnp.where(member == 0, od_own, od_back).reshape(rows, heads // 2, 2, HD)
    hi = jnp.where(member == 0, od_back, od_own).reshape(rows, heads // 2, 2, HD)
    od = jnp.concatenate([lo, hi], axis=1)
    attn_out = od[:, :, 0].reshape(1, rows, columns)
    query_grad = od[:, :, 1].reshape(1, rows, columns)
    return attn_out, query_grad, context_grad[None], weight_grad


def solution(mesh):
    return jax.shard_map(
        local,
        mesh=mesh,
        in_specs=(
            P("tower", "seq", "mp"),
            P("tower", "seq", None),
            P("tower", None, None, "mp"),
            P("tower", "seq", None),
            P("tower", "seq", "mp"),
        ),
        out_specs=(
            P("tower", "seq", "mp"),
            P("tower", "seq", "mp"),
            P("tower", "seq", None),
            P("tower", "seq", None, "mp"),
        ),
        check_vma=False,
    )
```

```python
import functools

import jax
import jax.numpy as jnp
from jax import lax
from jax.experimental import pallas as pl
from jax.experimental.pallas import tpu as pltpu
from jax.sharding import PartitionSpec as P

HD = 128
REACH = 2
NEG_FILL = -1e30
F32, BF16 = jnp.float32, jnp.bfloat16
ZS, YS, XS = 2, 4, 4
PAIR = 2
WINDOW = 6


def moved(value, axis, pairs):
    return lax.ppermute(value, axis, pairs)


def swapped(value, axis):
    return moved(value, axis, [(0, 1), (1, 0)])


def moved_across(value, pairs):
    both = [
        (tower * ZS * YS * XS + source, (1 - tower) * ZS * YS * XS + target)
        for tower in range(2)
        for source, target in pairs
    ]
    return lax.ppermute(value, ("tower", "seq"), both)


def seq_pairs(to):
    pairs = []
    for source in range(ZS * YS * XS):
        row, x = to(source // XS, source % XS)
        if 0 <= row < ZS * YS:
            pairs.append((source, row * XS + x))
    return pairs


def across_z():
    return seq_pairs(lambda row, x: ((row + YS) % (ZS * YS), x))


def in_row(flip):
    return seq_pairs(lambda row, x: (row, x ^ flip))


def next_row(back, flip):
    return seq_pairs(lambda row, x: (row + (1 if (x >= PAIR) != back else -1), x ^ flip))


def dot(a, b, dims):
    return lax.dot_general(a, b, ((dims[0], dims[1]), ((), ())), preferred_element_type=F32)


def projection_kernel(context, weight, kv, weight_out, total):
    step = pl.program_id(0)
    sides = jnp.swapaxes(weight[...], 0, 1)
    heads = sides.shape[2] // HD
    block = jnp.concatenate(
        [sides[side, :, h * HD : (h + 1) * HD] for h in range(heads) for side in range(2)], axis=1
    )
    weight_out[...] = block
    part = dot(context[...], block, ((1,), (0,)))

    @pl.when(step == 0)
    def _():
        total[...] = part

    @pl.when(step > 0)
    def _():
        total[...] += part

    @pl.when(step == pl.num_programs(0) - 1)
    def _():
        kv[...] = total[...].astype(BF16)


def projection(context, weight):
    rows, width = context.shape
    columns = weight.shape[2]
    depth = width // 4
    return pl.pallas_call(
        projection_kernel,
        out_shape=[
            jax.ShapeDtypeStruct((rows, 2 * columns), BF16),
            jax.ShapeDtypeStruct((width, 2 * columns), BF16),
        ],
        grid=(width // depth,),
        in_specs=[
            pl.BlockSpec((rows, depth), lambda i: (0, i)),
            pl.BlockSpec((depth, 2, columns), lambda i: (i, 0, 0)),
        ],
        out_specs=[
            pl.BlockSpec((rows, 2 * columns), lambda i: (0, 0)),
            pl.BlockSpec((depth, 2 * columns), lambda i: (i, 0)),
        ],
        scratch_shapes=[pltpu.VMEM((rows, 2 * columns), F32)],
        compiler_params=pltpu.CompilerParams(vmem_limit_bytes=60 * 2**20),
        cost_estimate=pl.CostEstimate(
            flops=4 * rows * width * columns, bytes_accessed=40 * 2**20, transcendentals=0
        ),
        name="projection",
    )(context, weight)


def attention_kernel(meta, q_a, c_a, q_b, c_b, *refs):
    kv_refs, (od_a, od_b), g_refs = refs[:6], refs[6:8], refs[8:11]
    kv_s, q_s, c_s, g_s = refs[11:]
    rows, heads = q_a.shape[0], od_a.shape[1] // (2 * HD)
    member, side = meta[0], meta[6]
    scale = HD ** (-0.5)
    near, far = 4 * side, 4 * (1 - side)
    order = (near + member, near + 1 - member, 2 + member, 3 - member, far + member, far + 1 - member)
    for ref, place in zip(kv_refs, order):
        kv_s[pl.ds(pl.multiple_of(place * rows, rows), rows), :] = ref[...]
    for ref, other, scratch in ((q_a, q_b, q_s), (c_a, c_b, c_s)):
        scratch[pl.ds(pl.multiple_of(member * rows, rows), rows), :] = ref[...]
        scratch[pl.ds(pl.multiple_of((1 - member) * rows, rows), rows), :] = other[...]
    g_s[...] = jnp.zeros_like(g_s)
    span = 2 * REACH + 1
    for i in range(PAIR):
        q = q_s[i * rows : (i + 1) * rows, :]
        c = c_s[i * rows : (i + 1) * rows, :]
        window = slice(i * rows, (i + span) * rows)
        keys = kv_s[window, :HD]
        values = kv_s[window, HD:]
        low, high = meta[2 + 2 * i], meta[3 + 2 * i]
        scores = dot(keys, q, ((1,), (1,))) * scale
        blocks = []
        for j in range(span):
            shard = meta[1] + i + j
            keep = (shard >= low) & (shard <= high)
            blocks.append(jnp.where(keep, scores[j * rows : (j + 1) * rows], NEG_FILL))
        scores = jnp.concatenate(blocks, axis=0)
        expo = jnp.exp(scores - jnp.max(scores, axis=0, keepdims=True))
        probs = expo * (1.0 / jnp.sum(expo, axis=0, keepdims=True))
        rounded = probs.astype(BF16)
        dprobs = dot(values, c, ((1,), (1,)))
        delta = jnp.sum(dprobs * probs, axis=0, keepdims=True)
        dscores = (probs * (dprobs - delta) * scale).astype(BF16)
        out = dot(values, rounded, ((0,), (0,)))
        dq = dot(keys, dscores, ((0,), (0,)))
        g_s[window, :HD] += dot(dscores, q, ((1,), (0,)))
        g_s[window, HD:] += dot(rounded, c, ((1,), (0,)))
        head = pl.program_id(0)
        parts = [
            (value.T.astype(BF16), pl.ds(pl.multiple_of((side_ * heads + head) * HD, HD), HD))
            for side_, value in enumerate((out, dq))
        ]

        @pl.when(member == i)
        def _():
            for value, columns in parts:
                od_a[:, columns] = value

        @pl.when(member != i)
        def _():
            for value, columns in parts:
                od_b[:, columns] = value

    for index, place in enumerate(order):
        begin = index % PAIR * rows
        g_refs[index // PAIR][begin : begin + rows, :] = g_s[
            pl.ds(pl.multiple_of(place * rows, rows), rows), :
        ].astype(BF16)


def attention(meta, qc_a, qc_b, kv_blocks):
    rows, half = kv_blocks[0].shape[0], qc_a.shape[1]
    heads = half // (2 * HD)
    one = lambda of: pl.BlockSpec((rows, HD), of)
    two = lambda of: pl.BlockSpec((rows, 2 * HD), of)
    plain = two(lambda h, m: (0, h))
    query, cot = one(lambda h, m: (0, h)), one(lambda h, m: (0, heads + h))
    shape = jax.ShapeDtypeStruct((rows, half), BF16)
    pair_shape = jax.ShapeDtypeStruct((PAIR * rows, half), BF16)
    whole = pl.BlockSpec((rows, half), lambda h, m: (0, 0))
    pair_block = pl.BlockSpec((PAIR * rows, 2 * HD), lambda h, m: (0, h))
    work = 2 * heads * rows * rows * 5
    return pl.pallas_call(
        attention_kernel,
        out_shape=[shape] * 2 + [pair_shape] * 3,
        grid_spec=pltpu.PrefetchScalarGridSpec(
            num_scalar_prefetch=1,
            grid=(heads,),
            in_specs=[query, cot, query, cot] + [plain] * 6,
            out_specs=[whole] * 2 + [pair_block] * 3,
            scratch_shapes=[
                pltpu.VMEM((WINDOW * rows, 2 * HD), BF16),
                pltpu.VMEM((PAIR * rows, HD), BF16),
                pltpu.VMEM((PAIR * rows, HD), BF16),
                pltpu.VMEM((WINDOW * rows, 2 * HD), F32),
            ],
        ),
        compiler_params=pltpu.CompilerParams(vmem_limit_bytes=62 * 2**20),
        cost_estimate=pl.CostEstimate(
            flops=work * 10 * HD, bytes_accessed=8 * 2**20, transcendentals=work
        ),
        name="attention",
    )(meta, qc_a, qc_a, qc_b, qc_b, *kv_blocks)


def weight_kernel(own, own_z, pair, pair_z, grad, grad_z, out):
    rows = own.shape[0]
    total = dot(own[...], grad[:rows, :], ((0,), (0,)))
    total += dot(pair[...], grad[rows:, :], ((0,), (0,)))
    total += dot(own_z[...], grad_z[:rows, :], ((0,), (0,)))
    total += dot(pair_z[...], grad_z[rows:, :], ((0,), (0,)))
    out[...] = total.astype(BF16)


def weight_partial(contexts, grads):
    rows, width = contexts[0].shape
    columns = grads[0].shape[1]
    split = 4
    block = width // split
    return pl.pallas_call(
        weight_kernel,
        out_shape=jax.ShapeDtypeStruct((width, columns), BF16),
        grid=(split,),
        in_specs=[pl.BlockSpec((v.shape[0], block), lambda i: (0, i)) for v in contexts]
        + [pl.BlockSpec(g.shape, lambda i: (0, 0)) for g in grads],
        out_specs=pl.BlockSpec((block, columns), lambda i: (i, 0)),
        compiler_params=pltpu.CompilerParams(vmem_limit_bytes=24 * 2**20),
        cost_estimate=pl.CostEstimate(
            flops=8 * rows * width * columns, bytes_accessed=8 * 2**20, transcendentals=0
        ),
        name="weight_partial",
    )(*contexts, *grads)


def context_kernel(grad, weight, out):
    out[...] = dot(grad[...], weight[...], ((1,), (1,))).astype(BF16)


def context_partial(grad, weight):
    rows, columns = grad.shape
    width = weight.shape[0]
    block = width // 4
    return pl.pallas_call(
        context_kernel,
        out_shape=jax.ShapeDtypeStruct((rows, width), BF16),
        grid=(width // block,),
        in_specs=[
            pl.BlockSpec((rows, columns), lambda i: (0, 0)),
            pl.BlockSpec((block, columns), lambda i: (i, 0)),
        ],
        out_specs=pl.BlockSpec((rows, block), lambda i: (0, i)),
        compiler_params=pltpu.CompilerParams(vmem_limit_bytes=60 * 2**20),
        cost_estimate=pl.CostEstimate(
            flops=2 * rows * width * columns, bytes_accessed=12 * 2**20, transcendentals=0
        ),
        name="context_partial",
    )(grad, weight)


def local(queries, context, kv_weight, spans, cotangent):
    queries, context, cotangent = queries[0], context[0], cotangent[0]
    rows, columns = queries.shape
    heads = columns // HD
    width = context.shape[1]
    position = lax.axis_index("seq")
    member = position % PAIR
    side = position % XS // PAIR
    z = position // (XS * YS)
    same_x, cross_x, pair_x = in_row(2), in_row(3), in_row(1)
    half_of = lambda v, which: lax.dynamic_slice_in_dim(
        v, which * (v.shape[1] // 2), v.shape[1] // 2, axis=1
    )
    in_order = lambda mine, other: jnp.concatenate(
        [jnp.where(member == 0, mine, other), jnp.where(member == 0, other, mine)], axis=1
    )
    total = lambda parts: functools.reduce(jnp.add, [p.astype(F32) for p in parts])

    span_rows = jnp.broadcast_to(jnp.pad(spans[0].astype(BF16), ((0, 0), (0, columns - 2))), (16, columns))
    qc_of = lambda which: jnp.concatenate(
        [
            jnp.concatenate([half_of(queries, which), half_of(cotangent, which)], axis=1),
            span_rows,
        ],
        axis=0,
    )
    qc_a = moved(qc_of(member), "seq", same_x)
    qc_b = moved(qc_of(1 - member), "seq", cross_x)

    local_kv, weight = projection(context, kv_weight[0])
    local_kv, qc_a, qc_b = lax.optimization_barrier((local_kv, qc_a, qc_b))
    same_half, next_half = half_of(local_kv, member), half_of(local_kv, 1 - member)
    kv_blocks = [
        swapped(same_half, "tower"),
        moved_across(next_half, pair_x),
        moved_across(same_half, same_x),
        moved_across(next_half, cross_x),
        moved_across(same_half, next_row(False, 0)),
        moved_across(next_half, next_row(False, 1)),
    ]
    ctx_own = half_of(context, z)
    kv_blocks, late_own, late_context = lax.optimization_barrier((kv_blocks, ctx_own, context))
    ctx_z = moved(half_of(late_context, 1 - z), "seq", across_z())
    ctx_pair = moved(late_own, "seq", pair_x)

    span_a, span_b = qc_a[rows, :2].astype(jnp.int32), qc_b[rows, :2].astype(jnp.int32)
    first = jnp.where(member == 0, span_a, span_b)
    second = jnp.where(member == 0, span_b, span_a)
    base = position - member - 4 * side
    meta = jnp.concatenate([jnp.stack([member, base]), first, second, side[None]]).astype(jnp.int32)
    od_a, od_b, g_near, g_mid, g_far = attention(meta, qc_a, qc_b, kv_blocks)

    g_mid = moved_across(g_mid, same_x)
    g_far, ctx_pair, ctx_z = lax.optimization_barrier((g_far, ctx_pair, ctx_z))
    g_far = moved_across(g_far, next_row(True, 0))
    returned = total([swapped(g_near, "tower"), g_mid, g_far]).astype(BF16)
    late_z, _ = lax.optimization_barrier((ctx_z, returned))
    ctx_pair_z = moved(late_z, "seq", pair_x)
    returned_z = moved(returned, "seq", across_z())
    other_rows = moved(returned[rows:], "seq", pair_x)
    od_a, od_b, _ = lax.optimization_barrier((od_a, od_b, returned))
    od_a, od_b = moved(od_a, "seq", same_x), moved(od_b, "seq", cross_x)
    other_rows, od_b = lax.optimization_barrier((other_rows, od_b))
    own_shard = in_order(returned[:rows], other_rows)
    partial_ctx = context_partial(own_shard, weight)
    sum_parts = [partial_ctx[:, : width // 3], partial_ctx[:, width // 3 :]]
    sum_first = swapped(sum_parts[0], "mp")


    partial_w = weight_partial([ctx_own, ctx_z, ctx_pair, ctx_pair_z], [returned, returned_z])
    partial_w, sum_first = lax.optimization_barrier((partial_w, sum_first))
    late_half, _ = lax.optimization_barrier((sum_parts[1], sum_first))
    sum_second = swapped(late_half, "mp")
    groups = [
        [(z_ * YS + y) * XS + PAIR * s + m for y in range(YS) for s in range(XS // PAIR)]
        for z_ in range(ZS)
        for m in range(PAIR)
    ]
    parts = lax.all_to_all(
        partial_w.reshape(len(groups[0]), -1, columns), "seq", 0, 0, axis_index_groups=groups
    )
    half_grad = jnp.sum(parts.astype(F32), axis=0).astype(BF16).reshape(PAIR, -1, columns)
    own_rows = lax.dynamic_index_in_dim(half_grad, member, 0, keepdims=False)
    pair_rows = lax.dynamic_index_in_dim(half_grad, 1 - member, 0, keepdims=False)
    weight_grad = (
        in_order(own_rows, moved(pair_rows, "seq", pair_x))
        .reshape(-1, heads, 2, HD)
        .transpose(0, 2, 1, 3)
        .reshape(1, -1, 2, columns)
    )

    context_grad = jnp.concatenate(
        [
            total([mine, other]).astype(BF16)
            for mine, other in zip(sum_parts, (sum_first, sum_second))
        ],
        axis=1,
    )
    attn_out = in_order(od_a[:, : columns // 2], od_b[:, : columns // 2])
    query_grad = in_order(od_a[:, columns // 2 :], od_b[:, columns // 2 :])
    return attn_out[None], query_grad[None], context_grad[None], weight_grad


def solution(mesh):
    return jax.shard_map(
        local,
        mesh=mesh,
        in_specs=(
            P("tower", "seq", "mp"),
            P("tower", "seq", None),
            P("tower", None, None, "mp"),
            P("tower", "seq", None),
            P("tower", "seq", "mp"),
        ),
        out_specs=(
            P("tower", "seq", "mp"),
            P("tower", "seq", "mp"),
            P("tower", "seq", None),
            P("tower", "seq", None, "mp"),
        ),
        check_vma=False,
    )
```

```python
import functools

import jax
import jax.numpy as jnp
from jax import lax
from jax.experimental import pallas as pl
from jax.experimental.pallas import tpu as pltpu
from jax.sharding import PartitionSpec as P

HD = 128
REACH = 2
NEG_FILL = -1e30
LOG2E = 1.4426950408889634
F32, BF16 = jnp.float32, jnp.bfloat16
ZS, YS, XS = 2, 4, 4
PAIR = 2
WINDOW = 6


def moved(value, axis, pairs):
    return lax.ppermute(value, axis, pairs)


def swapped(value, axis):
    return moved(value, axis, [(0, 1), (1, 0)])


def moved_across(value, pairs):
    both = [
        (tower * ZS * YS * XS + source, (1 - tower) * ZS * YS * XS + target)
        for tower in range(2)
        for source, target in pairs
    ]
    return lax.ppermute(value, ("tower", "seq"), both)


def seq_pairs(to):
    pairs = []
    for source in range(ZS * YS * XS):
        row, x = to(source // XS, source % XS)
        if 0 <= row < ZS * YS:
            pairs.append((source, row * XS + x))
    return pairs


def across_z():
    return seq_pairs(lambda row, x: ((row + YS) % (ZS * YS), x))


def in_row(flip):
    return seq_pairs(lambda row, x: (row, x ^ flip))


def next_row(back, flip):
    return seq_pairs(lambda row, x: (row + (1 if (x >= PAIR) != back else -1), x ^ flip))


def dot(a, b, dims):
    return lax.dot_general(a, b, ((dims[0], dims[1]), ((), ())), preferred_element_type=F32)


def projection_kernel(which, context, weight, kv, weight_out, total):
    step = pl.program_id(0)
    sides = jnp.swapaxes(weight[...], 0, 1)
    heads = sides.shape[2] // HD
    block = jnp.concatenate(
        [sides[side, :, h * HD : (h + 1) * HD] for h in range(heads) for side in range(2)], axis=1
    )
    weight_out[...] = block
    part = dot(context[...], block, ((1,), (0,)))

    @pl.when(step == 0)
    def _():
        total[...] = part

    @pl.when(step > 0)
    def _():
        total[...] += part

    @pl.when(step == pl.num_programs(0) - 1)
    def _():
        kv[...] = total[...].astype(BF16)


def projection(which, context, weight):
    rows, width = context.shape
    columns = weight.shape[2] // 2
    depth = width // 3
    return pl.pallas_call(
        projection_kernel,
        out_shape=[
            jax.ShapeDtypeStruct((rows, 2 * columns), BF16),
            jax.ShapeDtypeStruct((width, 2 * columns), BF16),
        ],
        grid_spec=pltpu.PrefetchScalarGridSpec(
            num_scalar_prefetch=1,
            grid=(width // depth,),
            in_specs=[
                pl.BlockSpec((rows, depth), lambda i, w: (0, i)),
                pl.BlockSpec((depth, 2, columns), lambda i, w: (i, 0, w[0])),
            ],
            out_specs=[
                pl.BlockSpec((rows, 2 * columns), lambda i, w: (0, 0)),
                pl.BlockSpec((depth, 2 * columns), lambda i, w: (i, 0)),
            ],
            scratch_shapes=[pltpu.VMEM((rows, 2 * columns), F32)],
        ),
        compiler_params=pltpu.CompilerParams(vmem_limit_bytes=60 * 2**20),
        cost_estimate=pl.CostEstimate(
            flops=4 * rows * width * columns, bytes_accessed=20 * 2**20, transcendentals=0
        ),
        name="projection",
    )(which.reshape(1), context, weight)


def attention_kernel(meta, q_a, c_a, q_b, c_b, *refs):
    kv_refs, (od_a, od_b), g_refs = refs[:6], refs[6:8], refs[8:11]
    kv_s, q_s, c_s, g_s = refs[11:]
    rows, heads = q_a.shape[0], od_a.shape[1] // (2 * HD)
    member, side = meta[0], meta[6]
    scale = HD ** (-0.5)
    unit = scale * LOG2E
    results = []
    near, far = 4 * side, 4 * (1 - side)
    order = (near + member, near + 1 - member, 2 + member, 3 - member, far + member, far + 1 - member)
    for ref, place in zip(kv_refs, order):
        kv_s[pl.ds(pl.multiple_of(place * rows, rows), rows), :] = ref[...]
    for ref, other, scratch in ((q_a, q_b, q_s), (c_a, c_b, c_s)):
        scratch[pl.ds(pl.multiple_of(member * rows, rows), rows), :] = ref[...]
        scratch[pl.ds(pl.multiple_of((1 - member) * rows, rows), rows), :] = other[...]
    g_s[...] = jnp.zeros_like(g_s)
    span = 2 * REACH + 1
    for i in range(PAIR):
        q = q_s[i * rows : (i + 1) * rows, :]
        c = c_s[i * rows : (i + 1) * rows, :]
        window = slice(i * rows, (i + span) * rows)
        keys = kv_s[window, :HD]
        values = kv_s[window, HD:]
        low, high = meta[2 + 2 * i], meta[3 + 2 * i]
        scores = dot(keys, q, ((1,), (1,)))
        block = lambda v, j: v[j * rows : (j + 1) * rows]
        offsets = []
        for j in range(span):
            shard = meta[1] + i + j
            offsets.append(jnp.where((shard >= low) & (shard <= high), 0.0, NEG_FILL))
        row_max = functools.reduce(
            jnp.maximum,
            [jnp.max(block(scores, j), axis=0, keepdims=True) + offsets[j] for j in range(span)],
        )
        expo = [
            jnp.exp2(block(scores, j) * unit + (offsets[j] - row_max * unit)) for j in range(span)
        ]
        norm = functools.reduce(jnp.add, [jnp.sum(e, axis=0, keepdims=True) for e in expo])
        probs = jnp.concatenate(expo, axis=0) * (1.0 / norm)
        rounded = probs.astype(BF16)
        dprobs = dot(values, c, ((1,), (1,)))
        delta = jnp.sum(dprobs * probs, axis=0, keepdims=True)
        dscores = (probs * (dprobs - delta)).astype(BF16)
        out = dot(values, rounded, ((0,), (0,)))
        dq = dot(keys, dscores, ((0,), (0,))) * scale
        g_s[window, :HD] += dot(dscores, q, ((1,), (0,)))
        g_s[window, HD:] += dot(rounded, c, ((1,), (0,)))
        results.append([value.T.astype(BF16) for value in (out, dq)])
    head = pl.program_id(0)
    for part, (first, second) in enumerate(zip(*results)):
        columns = pl.ds(pl.multiple_of((part * heads + head) * HD, HD), HD)
        od_a[:, columns] = jnp.where(member == 0, first, second)
        od_b[:, columns] = jnp.where(member == 0, second, first)
    g_s[:, :HD] *= scale

    for index, place in enumerate(order):
        begin = index % PAIR * rows
        g_refs[index // PAIR][begin : begin + rows, :] = g_s[
            pl.ds(pl.multiple_of(place * rows, rows), rows), :
        ].astype(BF16)


def attention(meta, qc_a, qc_b, kv_blocks):
    rows, half = kv_blocks[0].shape[0], qc_a.shape[1]
    heads = half // (2 * HD)
    one = lambda of: pl.BlockSpec((rows, HD), of)
    two = lambda of: pl.BlockSpec((rows, 2 * HD), of)
    plain = two(lambda h, m: (0, h))
    query, cot = one(lambda h, m: (0, h)), one(lambda h, m: (0, heads + h))
    shape = jax.ShapeDtypeStruct((rows, half), BF16)
    pair_shape = jax.ShapeDtypeStruct((PAIR * rows, half), BF16)
    whole = pl.BlockSpec((rows, half), lambda h, m: (0, 0))
    pair_block = pl.BlockSpec((PAIR * rows, 2 * HD), lambda h, m: (0, h))
    work = 2 * heads * rows * rows * 5
    return pl.pallas_call(
        attention_kernel,
        out_shape=[shape] * 2 + [pair_shape] * 3,
        grid_spec=pltpu.PrefetchScalarGridSpec(
            num_scalar_prefetch=1,
            grid=(heads,),
            in_specs=[query, cot, query, cot] + [plain] * 6,
            out_specs=[whole] * 2 + [pair_block] * 3,
            scratch_shapes=[
                pltpu.VMEM((WINDOW * rows, 2 * HD), BF16),
                pltpu.VMEM((PAIR * rows, HD), BF16),
                pltpu.VMEM((PAIR * rows, HD), BF16),
                pltpu.VMEM((WINDOW * rows, 2 * HD), F32),
            ],
        ),
        compiler_params=pltpu.CompilerParams(vmem_limit_bytes=62 * 2**20),
        cost_estimate=pl.CostEstimate(
            flops=work * 10 * HD, bytes_accessed=8 * 2**20, transcendentals=work
        ),
        name="attention",
    )(meta, qc_a, qc_a, qc_b, qc_b, *kv_blocks)


def weight_kernel(own, own_z, pair, pair_z, grad, grad_z, out):
    rows = own.shape[0]
    total = dot(own[...], grad[:rows, :], ((0,), (0,)))
    total += dot(pair[...], grad[rows:, :], ((0,), (0,)))
    total += dot(own_z[...], grad_z[:rows, :], ((0,), (0,)))
    total += dot(pair_z[...], grad_z[rows:, :], ((0,), (0,)))
    out[...] = total.astype(BF16)


def weight_partial(contexts, grads):
    rows, width = contexts[0].shape
    columns = grads[0].shape[1]
    split = 4
    block = width // split
    return pl.pallas_call(
        weight_kernel,
        out_shape=jax.ShapeDtypeStruct((width, columns), BF16),
        grid=(split,),
        in_specs=[pl.BlockSpec((v.shape[0], block), lambda i: (0, i)) for v in contexts]
        + [pl.BlockSpec(g.shape, lambda i: (0, 0)) for g in grads],
        out_specs=pl.BlockSpec((block, columns), lambda i: (i, 0)),
        compiler_params=pltpu.CompilerParams(vmem_limit_bytes=24 * 2**20),
        cost_estimate=pl.CostEstimate(
            flops=8 * rows * width * columns, bytes_accessed=8 * 2**20, transcendentals=0
        ),
        name="weight_partial",
    )(*contexts, *grads)


def context_kernel(grad, grad_next, weight, weight_next, out):
    total = dot(grad[...], weight[...], ((1,), (1,)))
    total += dot(grad_next[...], weight_next[...], ((1,), (1,)))
    out[...] = total.astype(BF16)


def context_partial(returned, other_rows, weight_same, weight_next):
    rows, columns = other_rows.shape
    width = weight_same.shape[0]
    block = width // 4
    grad = pl.BlockSpec((rows, columns), lambda i: (0, 0))
    weight = pl.BlockSpec((block, columns), lambda i: (i, 0))
    return pl.pallas_call(
        context_kernel,
        out_shape=jax.ShapeDtypeStruct((rows, width), BF16),
        grid=(width // block,),
        in_specs=[grad, grad, weight, weight],
        out_specs=pl.BlockSpec((rows, block), lambda i: (0, i)),
        compiler_params=pltpu.CompilerParams(vmem_limit_bytes=60 * 2**20),
        cost_estimate=pl.CostEstimate(
            flops=4 * rows * width * columns, bytes_accessed=12 * 2**20, transcendentals=0
        ),
        name="context_partial",
    )(returned, other_rows, weight_same, weight_next)


def local(queries, context, kv_weight, spans, cotangent):
    queries, context, cotangent = queries[0], context[0], cotangent[0]
    rows, columns = queries.shape
    heads = columns // HD
    width = context.shape[1]
    position = lax.axis_index("seq")
    member = position % PAIR
    side = position % XS // PAIR
    z = position // (XS * YS)
    same_x, cross_x, pair_x = in_row(2), in_row(3), in_row(1)
    half_of = lambda v, which: lax.dynamic_slice_in_dim(
        v, which * (v.shape[1] // 2), v.shape[1] // 2, axis=1
    )
    in_order = lambda mine, other: jnp.concatenate(
        [jnp.where(member == 0, mine, other), jnp.where(member == 0, other, mine)], axis=1
    )
    total = lambda parts: functools.reduce(jnp.add, [p.astype(F32) for p in parts])

    span_rows = jnp.broadcast_to(jnp.pad(spans[0].astype(BF16), ((0, 0), (0, columns - 2))), (16, columns))
    qc_of = lambda which: jnp.concatenate(
        [
            jnp.concatenate([half_of(queries, which), half_of(cotangent, which)], axis=1),
            span_rows,
        ],
        axis=0,
    )
    qc_a = moved(qc_of(member), "seq", same_x)
    qc_b = moved(qc_of(1 - member), "seq", cross_x)

    next_half, weight_next = projection(1 - member, context, kv_weight[0])
    late_context, _ = lax.optimization_barrier((context, next_half))
    same_half, weight_same = projection(member, late_context, kv_weight[0])
    same_half, qc_a, qc_b = lax.optimization_barrier((same_half, qc_a, qc_b))
    kv_blocks = [
        swapped(same_half, "tower"),
        moved_across(next_half, pair_x),
        moved_across(same_half, same_x),
        moved_across(next_half, cross_x),
        moved_across(same_half, next_row(False, 0)),
        moved_across(next_half, next_row(False, 1)),
    ]
    ctx_own = half_of(context, z)
    kv_blocks, late_own, ctx_rest = lax.optimization_barrier(
        (kv_blocks, ctx_own, half_of(context, 1 - z))
    )
    ctx_z = moved(ctx_rest, "seq", across_z())
    ctx_pair = moved(late_own, "seq", pair_x)

    span_a, span_b = qc_a[rows, :2].astype(jnp.int32), qc_b[rows, :2].astype(jnp.int32)
    first = jnp.where(member == 0, span_a, span_b)
    second = jnp.where(member == 0, span_b, span_a)
    base = position - member - 4 * side
    meta = jnp.concatenate([jnp.stack([member, base]), first, second, side[None]]).astype(jnp.int32)
    od_a, od_b, g_near, g_mid, g_far = attention(meta, qc_a, qc_b, kv_blocks)

    g_mid = moved_across(g_mid, same_x)
    g_near, ctx_pair, ctx_z = lax.optimization_barrier((g_near, ctx_pair, ctx_z))
    g_far = moved_across(g_far, next_row(True, 0))
    returned = total([swapped(g_near, "tower"), g_mid, g_far]).astype(BF16)
    late_z, _ = lax.optimization_barrier((ctx_z, returned))
    ctx_pair_z = moved(late_z, "seq", pair_x)
    returned_z = moved(returned, "seq", across_z())
    other_rows = moved(returned[rows:], "seq", pair_x)
    od_b, _ = lax.optimization_barrier((od_b, returned))
    od_b = moved(od_b, "seq", cross_x)
    other_rows, od_b = lax.optimization_barrier((other_rows, od_b))
    partial_ctx = context_partial(returned, other_rows, weight_same, weight_next)
    od_a, _ = lax.optimization_barrier((od_a, partial_ctx))
    od_a = moved(od_a, "seq", same_x)
    sum_parts = [partial_ctx[:, : width // 3], partial_ctx[:, width // 3 :]]
    sum_first = swapped(sum_parts[0], "mp")


    partial_w = weight_partial([ctx_own, ctx_z, ctx_pair, ctx_pair_z], [returned, returned_z])
    partial_w, sum_first, od_a = lax.optimization_barrier((partial_w, sum_first, od_a))
    late_half, _ = lax.optimization_barrier((sum_parts[1], sum_first))
    sum_second = swapped(late_half, "mp")
    plane = YS * XS
    groups = [[z_ * plane + i for i in range(plane)] for z_ in range(ZS)]
    parts = lax.all_to_all(
        partial_w.reshape(plane, -1, columns), "seq", 0, 0, axis_index_groups=groups
    )
    weight_grad = (
        jnp.sum(parts.reshape(plane // PAIR, PAIR, -1, columns).astype(F32), axis=0)
        .astype(BF16)
        .reshape(PAIR, -1, heads // PAIR, 2, HD)
        .transpose(1, 3, 0, 2, 4)
        .reshape(1, -1, 2, columns)
    )

    context_grad = jnp.concatenate(
        [
            total([mine, other]).astype(BF16)
            for mine, other in zip(sum_parts, (sum_first, sum_second))
        ],
        axis=1,
    )
    attn_out = in_order(od_a[:, : columns // 2], od_b[:, : columns // 2])
    query_grad = in_order(od_a[:, columns // 2 :], od_b[:, columns // 2 :])
    return attn_out[None], query_grad[None], context_grad[None], weight_grad


def solution(mesh):
    return jax.shard_map(
        local,
        mesh=mesh,
        in_specs=(
            P("tower", "seq", "mp"),
            P("tower", "seq", None),
            P("tower", None, None, "mp"),
            P("tower", "seq", None),
            P("tower", "seq", "mp"),
        ),
        out_specs=(
            P("tower", "seq", "mp"),
            P("tower", "seq", "mp"),
            P("tower", "seq", None),
            P("tower", "seq", None, "mp"),
        ),
        check_vma=False,
    )
```

```python
import functools

import jax
import jax.numpy as jnp
from jax import lax
from jax.experimental import pallas as pl
from jax.experimental.pallas import tpu as pltpu
from jax.sharding import PartitionSpec as P

HD = 128
REACH = 2
NEG_FILL = -1e30
LOG2E = 1.4426950408889634
F32, BF16 = jnp.float32, jnp.bfloat16
ZS, YS, XS = 2, 4, 4
PAIR = 2
WINDOW = 6


def moved(value, axis, pairs):
    return lax.ppermute(value, axis, pairs)


def swapped(value, axis):
    return moved(value, axis, [(0, 1), (1, 0)])


def moved_across(value, pairs):
    both = [
        (tower * ZS * YS * XS + source, (1 - tower) * ZS * YS * XS + target)
        for tower in range(2)
        for source, target in pairs
    ]
    return lax.ppermute(value, ("tower", "seq"), both)


def seq_pairs(to):
    pairs = []
    for source in range(ZS * YS * XS):
        row, x = to(source // XS, source % XS)
        if 0 <= row < ZS * YS:
            pairs.append((source, row * XS + x))
    return pairs


def across_z():
    return seq_pairs(lambda row, x: ((row + YS) % (ZS * YS), x))


def in_row(flip):
    return seq_pairs(lambda row, x: (row, x ^ flip))


def next_row(back, flip):
    return seq_pairs(lambda row, x: (row + (1 if (x >= PAIR) != back else -1), x ^ flip))


def dot(a, b, dims):
    return lax.dot_general(a, b, ((dims[0], dims[1]), ((), ())), preferred_element_type=F32)


def total_kernel(parts, out):
    columns = parts.shape[2]
    heads = columns // (2 * HD)
    for half in range(PAIR):
        total = parts[half].astype(F32)
        for source in range(half + PAIR, parts.shape[0], PAIR):
            total += parts[source].astype(F32)
        for h in range(heads):
            for side in range(2):
                begin = (2 * h + side) * HD
                place = side * columns + (half * heads + h) * HD
                out[:, place : place + HD] = total[:, begin : begin + HD].astype(BF16)


def weight_total(parts):
    rows, columns = parts.shape[1:]
    block = rows // 2
    return pl.pallas_call(
        total_kernel,
        out_shape=jax.ShapeDtypeStruct((rows, 2 * columns), BF16),
        grid=(rows // block,),
        in_specs=[pl.BlockSpec((parts.shape[0], block, columns), lambda i: (0, i, 0))],
        out_specs=pl.BlockSpec((block, 2 * columns), lambda i: (i, 0)),
        compiler_params=pltpu.CompilerParams(vmem_limit_bytes=24 * 2**20),
        name="weight_total",
    )(parts)


def head_columns(weight):
    sides = jnp.swapaxes(weight, 0, 1)
    heads = sides.shape[2] // HD
    return jnp.concatenate(
        [sides[side, :, h * HD : (h + 1) * HD] for h in range(heads) for side in range(2)], axis=1
    )


def projection_kernel(which, context, weight, kv, total):
    step = pl.program_id(0)
    part = dot(context[...], head_columns(weight[...]), ((1,), (0,)))

    @pl.when(step == 0)
    def _():
        total[...] = part

    @pl.when(step > 0)
    def _():
        total[...] += part

    @pl.when(step == pl.num_programs(0) - 1)
    def _():
        kv[...] = total[...].astype(BF16)


def projection(which, context, weight):
    rows, width = context.shape
    columns = weight.shape[2] // 2
    depth = width // 3
    return pl.pallas_call(
        projection_kernel,
        out_shape=jax.ShapeDtypeStruct((rows, 2 * columns), BF16),
        grid_spec=pltpu.PrefetchScalarGridSpec(
            num_scalar_prefetch=1,
            grid=(width // depth,),
            in_specs=[
                pl.BlockSpec((rows, depth), lambda i, w: (0, i)),
                pl.BlockSpec((depth, 2, columns), lambda i, w: (i, 0, w[0])),
            ],
            out_specs=pl.BlockSpec((rows, 2 * columns), lambda i, w: (0, 0)),
            scratch_shapes=[pltpu.VMEM((rows, 2 * columns), F32)],
        ),
        compiler_params=pltpu.CompilerParams(vmem_limit_bytes=56 * 2**20),
        cost_estimate=pl.CostEstimate(
            flops=4 * rows * width * columns, bytes_accessed=20 * 2**20, transcendentals=0
        ),
        name="projection",
    )(which.reshape(1), context, weight)


def attention_kernel(meta, q_a, c_a, q_b, c_b, *refs):
    kv_refs, (od_a, od_b), g_refs = refs[:6], refs[6:8], refs[8:11]
    kv_s, q_s, c_s, g_s = refs[11:]
    rows, heads = q_a.shape[0], od_a.shape[1] // (2 * HD)
    member, side = meta[0], meta[6]
    scale = HD ** (-0.5)
    unit = scale * LOG2E
    results = []
    near, far = 4 * side, 4 * (1 - side)
    order = (near + member, near + 1 - member, 2 + member, 3 - member, far + member, far + 1 - member)
    for ref, place in zip(kv_refs, order):
        kv_s[pl.ds(pl.multiple_of(place * rows, rows), rows), :] = ref[...]
    for ref, other, scratch in ((q_a, q_b, q_s), (c_a, c_b, c_s)):
        scratch[pl.ds(pl.multiple_of(member * rows, rows), rows), :] = ref[...]
        scratch[pl.ds(pl.multiple_of((1 - member) * rows, rows), rows), :] = other[...]
    g_s[...] = jnp.zeros_like(g_s)
    span = 2 * REACH + 1
    for i in range(PAIR):
        q = q_s[i * rows : (i + 1) * rows, :]
        c = c_s[i * rows : (i + 1) * rows, :]
        window = slice(i * rows, (i + span) * rows)
        keys = kv_s[window, :HD]
        values = kv_s[window, HD:]
        low, high = meta[2 + 2 * i], meta[3 + 2 * i]
        scores = dot(keys, q, ((1,), (1,)))
        block = lambda v, j: v[j * rows : (j + 1) * rows]
        offsets = []
        for j in range(span):
            shard = meta[1] + i + j
            offsets.append(jnp.where((shard >= low) & (shard <= high), 0.0, NEG_FILL))
        row_max = functools.reduce(
            jnp.maximum,
            [jnp.max(block(scores, j), axis=0, keepdims=True) + offsets[j] for j in range(span)],
        )
        expo = [
            jnp.exp2(block(scores, j) * unit + (offsets[j] - row_max * unit)) for j in range(span)
        ]
        norm = functools.reduce(jnp.add, [jnp.sum(e, axis=0, keepdims=True) for e in expo])
        probs = jnp.concatenate(expo, axis=0) * (1.0 / norm)
        rounded = probs.astype(BF16)
        dprobs = dot(values, c, ((1,), (1,)))
        delta = jnp.sum(dprobs * probs, axis=0, keepdims=True)
        dscores = (probs * (dprobs - delta)).astype(BF16)
        out = dot(values, rounded, ((0,), (0,)))
        dq = dot(keys, dscores, ((0,), (0,))) * scale
        g_s[window, :HD] += dot(dscores, q, ((1,), (0,)))
        g_s[window, HD:] += dot(rounded, c, ((1,), (0,)))
        results.append([value.T.astype(BF16) for value in (out, dq)])
    head = pl.program_id(0)
    for part, (first, second) in enumerate(zip(*results)):
        columns = pl.ds(pl.multiple_of((part * heads + head) * HD, HD), HD)
        od_a[:, columns] = jnp.where(member == 0, first, second)
        od_b[:, columns] = jnp.where(member == 0, second, first)
    g_s[:, :HD] *= scale

    for index, place in enumerate(order):
        begin = index % PAIR * rows
        g_refs[index // PAIR][begin : begin + rows, :] = g_s[
            pl.ds(pl.multiple_of(place * rows, rows), rows), :
        ].astype(BF16)


def attention(meta, qc_a, qc_b, kv_blocks):
    rows, half = kv_blocks[0].shape[0], qc_a.shape[1]
    heads = half // (2 * HD)
    one = lambda of: pl.BlockSpec((rows, HD), of)
    two = lambda of: pl.BlockSpec((rows, 2 * HD), of)
    plain = two(lambda h, m: (0, h))
    query, cot = one(lambda h, m: (0, h)), one(lambda h, m: (0, heads + h))
    shape = jax.ShapeDtypeStruct((rows, half), BF16)
    pair_shape = jax.ShapeDtypeStruct((PAIR * rows, half), BF16)
    whole = pl.BlockSpec((rows, half), lambda h, m: (0, 0))
    pair_block = pl.BlockSpec((PAIR * rows, 2 * HD), lambda h, m: (0, h))
    work = 2 * heads * rows * rows * 5
    return pl.pallas_call(
        attention_kernel,
        out_shape=[shape] * 2 + [pair_shape] * 3,
        grid_spec=pltpu.PrefetchScalarGridSpec(
            num_scalar_prefetch=1,
            grid=(heads,),
            in_specs=[query, cot, query, cot] + [plain] * 6,
            out_specs=[whole] * 2 + [pair_block] * 3,
            scratch_shapes=[
                pltpu.VMEM((WINDOW * rows, 2 * HD), BF16),
                pltpu.VMEM((PAIR * rows, HD), BF16),
                pltpu.VMEM((PAIR * rows, HD), BF16),
                pltpu.VMEM((WINDOW * rows, 2 * HD), F32),
            ],
        ),
        compiler_params=pltpu.CompilerParams(vmem_limit_bytes=56 * 2**20),
        cost_estimate=pl.CostEstimate(
            flops=work * 10 * HD, bytes_accessed=8 * 2**20, transcendentals=work
        ),
        name="attention",
    )(meta, qc_a, qc_a, qc_b, qc_b, *kv_blocks)


def weight_kernel(own, own_z, pair, pair_z, grad, grad_z, out):
    rows = own.shape[0]
    total = dot(own[...], grad[:rows, :], ((0,), (0,)))
    total += dot(pair[...], grad[rows:, :], ((0,), (0,)))
    total += dot(own_z[...], grad_z[:rows, :], ((0,), (0,)))
    total += dot(pair_z[...], grad_z[rows:, :], ((0,), (0,)))
    out[...] = total.astype(BF16)


def weight_partial(contexts, grads):
    rows, width = contexts[0].shape
    columns = grads[0].shape[1]
    split = 4
    block = width // split
    return pl.pallas_call(
        weight_kernel,
        out_shape=jax.ShapeDtypeStruct((width, columns), BF16),
        grid=(split,),
        in_specs=[pl.BlockSpec((v.shape[0], block), lambda i: (0, i)) for v in contexts]
        + [pl.BlockSpec(g.shape, lambda i: (0, 0)) for g in grads],
        out_specs=pl.BlockSpec((block, columns), lambda i: (i, 0)),
        compiler_params=pltpu.CompilerParams(vmem_limit_bytes=24 * 2**20),
        cost_estimate=pl.CostEstimate(
            flops=8 * rows * width * columns, bytes_accessed=8 * 2**20, transcendentals=0
        ),
        name="weight_partial",
    )(*contexts, *grads)


def context_kernel(member, grad, grad_next, weight, out, both):
    half = grad.shape[1]

    @pl.when(pl.program_id(0) == 0)
    def _():
        both[:, pl.ds(pl.multiple_of(member[0] * half, half), half)] = grad[...]
        both[:, pl.ds(pl.multiple_of((1 - member[0]) * half, half), half)] = grad_next[...]

    out[...] = dot(both[...], head_columns(weight[...]), ((1,), (1,))).astype(BF16)


def context_partial(member, returned, other_rows, weight):
    rows, columns = other_rows.shape
    width = weight.shape[0]
    block = width // 4
    grad = pl.BlockSpec((rows, columns), lambda i, m: (0, 0))
    return pl.pallas_call(
        context_kernel,
        out_shape=jax.ShapeDtypeStruct((rows, width), BF16),
        grid_spec=pltpu.PrefetchScalarGridSpec(
            num_scalar_prefetch=1,
            grid=(width // block,),
            in_specs=[grad, grad, pl.BlockSpec((block, 2, columns), lambda i, m: (i, 0, 0))],
            out_specs=pl.BlockSpec((rows, block), lambda i, m: (0, i)),
            scratch_shapes=[pltpu.VMEM((rows, 2 * columns), BF16)],
        ),
        compiler_params=pltpu.CompilerParams(vmem_limit_bytes=50 * 2**20),
        cost_estimate=pl.CostEstimate(
            flops=4 * rows * width * columns, bytes_accessed=12 * 2**20, transcendentals=0
        ),
        name="context_partial",
    )(member.reshape(1), returned, other_rows, weight)


def local(queries, context, kv_weight, spans, cotangent):
    queries, context, cotangent = queries[0], context[0], cotangent[0]
    rows, columns = queries.shape
    heads = columns // HD
    width = context.shape[1]
    position = lax.axis_index("seq")
    member = position % PAIR
    side = position % XS // PAIR
    z = position // (XS * YS)
    same_x, cross_x, pair_x = in_row(2), in_row(3), in_row(1)
    half_of = lambda v, which: lax.dynamic_slice_in_dim(
        v, which * (v.shape[1] // 2), v.shape[1] // 2, axis=1
    )
    in_order = lambda mine, other: jnp.concatenate(
        [jnp.where(member == 0, mine, other), jnp.where(member == 0, other, mine)], axis=1
    )
    total = lambda parts: functools.reduce(jnp.add, [p.astype(F32) for p in parts])

    span_rows = jnp.broadcast_to(jnp.pad(spans[0].astype(BF16), ((0, 0), (0, columns - 2))), (16, columns))
    qc_of = lambda which: jnp.concatenate(
        [
            jnp.concatenate([half_of(queries, which), half_of(cotangent, which)], axis=1),
            span_rows,
        ],
        axis=0,
    )
    qc_a = moved(qc_of(member), "seq", same_x)
    qc_b = moved(qc_of(1 - member), "seq", cross_x)

    next_half = projection(1 - member, context, kv_weight[0])
    late_context, _ = lax.optimization_barrier((context, next_half))
    same_half = projection(member, late_context, kv_weight[0])
    same_half, qc_a, qc_b = lax.optimization_barrier((same_half, qc_a, qc_b))
    kv_blocks = [
        swapped(same_half, "tower"),
        moved_across(next_half, pair_x),
        moved_across(same_half, same_x),
        moved_across(next_half, cross_x),
        moved_across(same_half, next_row(False, 0)),
        moved_across(next_half, next_row(False, 1)),
    ]
    ctx_own = half_of(context, z)
    kv_blocks, late_own, ctx_rest = lax.optimization_barrier(
        (kv_blocks, ctx_own, half_of(context, 1 - z))
    )
    ctx_z = moved(ctx_rest, "seq", across_z())
    ctx_pair = moved(late_own, "seq", pair_x)

    span_a, span_b = qc_a[rows, :2].astype(jnp.int32), qc_b[rows, :2].astype(jnp.int32)
    first = jnp.where(member == 0, span_a, span_b)
    second = jnp.where(member == 0, span_b, span_a)
    base = position - member - 4 * side
    meta = jnp.concatenate([jnp.stack([member, base]), first, second, side[None]]).astype(jnp.int32)
    od_a, od_b, g_near, g_mid, g_far = attention(meta, qc_a, qc_b, kv_blocks)

    g_mid = moved_across(g_mid, same_x)
    g_near, ctx_pair, ctx_z = lax.optimization_barrier((g_near, ctx_pair, ctx_z))
    g_far = moved_across(g_far, next_row(True, 0))
    returned = total([swapped(g_near, "tower"), g_mid, g_far]).astype(BF16)
    late_z, _ = lax.optimization_barrier((ctx_z, returned))
    ctx_pair_z = moved(late_z, "seq", pair_x)
    returned_z = moved(returned, "seq", across_z())
    other_rows = moved(returned[rows:], "seq", pair_x)
    od_b, _ = lax.optimization_barrier((od_b, returned))
    od_b = moved(od_b, "seq", cross_x)
    other_rows, od_b = lax.optimization_barrier((other_rows, od_b))
    partial_ctx = context_partial(member, returned, other_rows, kv_weight[0])
    od_a, _ = lax.optimization_barrier((od_a, partial_ctx))
    od_a = moved(od_a, "seq", same_x)
    sum_parts = [partial_ctx[:, : width // 3], partial_ctx[:, width // 3 :]]
    sum_first = swapped(sum_parts[0], "mp")


    partial_w = weight_partial([ctx_own, ctx_z, ctx_pair, ctx_pair_z], [returned, returned_z])
    partial_w, sum_first, od_a = lax.optimization_barrier((partial_w, sum_first, od_a))
    late_half, _ = lax.optimization_barrier((sum_parts[1], sum_first))
    sum_second = swapped(late_half, "mp")
    plane = YS * XS
    groups = [[z_ * plane + i for i in range(plane)] for z_ in range(ZS)]
    parts = lax.all_to_all(
        partial_w.reshape(plane, -1, columns), "seq", 0, 0, axis_index_groups=groups
    )
    weight_grad = weight_total(parts).reshape(-1, 2, columns)[None]

    context_grad = jnp.concatenate(
        [
            total([mine, other]).astype(BF16)
            for mine, other in zip(sum_parts, (sum_first, sum_second))
        ],
        axis=1,
    )
    attn_out = in_order(od_a[:, : columns // 2], od_b[:, : columns // 2])
    query_grad = in_order(od_a[:, columns // 2 :], od_b[:, columns // 2 :])
    return attn_out[None], query_grad[None], context_grad[None], weight_grad


def solution(mesh):
    return jax.shard_map(
        local,
        mesh=mesh,
        in_specs=(
            P("tower", "seq", "mp"),
            P("tower", "seq", None),
            P("tower", None, None, "mp"),
            P("tower", "seq", None),
            P("tower", "seq", "mp"),
        ),
        out_specs=(
            P("tower", "seq", "mp"),
            P("tower", "seq", "mp"),
            P("tower", "seq", None),
            P("tower", "seq", None, "mp"),
        ),
        check_vma=False,
    )
```

```python
import functools

import jax
import jax.numpy as jnp
from jax import lax
from jax.experimental import pallas as pl
from jax.experimental.pallas import tpu as pltpu
from jax.sharding import PartitionSpec as P

HD = 128
REACH = 2
NEG_FILL = -1e30
LOG2E = 1.4426950408889634
F32, BF16 = jnp.float32, jnp.bfloat16
ZS, YS, XS = 2, 4, 4
PAIR = 2
WINDOW = 6


def moved(value, axis, pairs):
    return lax.ppermute(value, axis, pairs)


def swapped(value, axis):
    return moved(value, axis, [(0, 1), (1, 0)])


def moved_across(value, pairs):
    both = [
        (tower * ZS * YS * XS + source, (1 - tower) * ZS * YS * XS + target)
        for tower in range(2)
        for source, target in pairs
    ]
    return lax.ppermute(value, ("tower", "seq"), both)


def seq_pairs(to):
    pairs = []
    for source in range(ZS * YS * XS):
        row, x = to(source // XS, source % XS)
        if 0 <= row < ZS * YS:
            pairs.append((source, row * XS + x))
    return pairs


def across_z():
    return seq_pairs(lambda row, x: ((row + YS) % (ZS * YS), x))


def in_row(flip):
    return seq_pairs(lambda row, x: (row, x ^ flip))


def next_row(back, flip):
    return seq_pairs(lambda row, x: (row + (1 if (x >= PAIR) != back else -1), x ^ flip))


def dot(a, b, dims):
    return lax.dot_general(a, b, ((dims[0], dims[1]), ((), ())), preferred_element_type=F32)


def total_kernel(parts, out):
    columns = parts.shape[2]
    heads = columns // (2 * HD)
    for half in range(PAIR):
        total = parts[half].astype(F32)
        for source in range(half + PAIR, parts.shape[0], PAIR):
            total += parts[source].astype(F32)
        for h in range(heads):
            for side in range(2):
                begin = (2 * h + side) * HD
                place = side * columns + (half * heads + h) * HD
                out[:, place : place + HD] = total[:, begin : begin + HD].astype(BF16)


def weight_total(parts):
    rows, columns = parts.shape[1:]
    block = rows // 2
    return pl.pallas_call(
        total_kernel,
        out_shape=jax.ShapeDtypeStruct((rows, 2 * columns), BF16),
        grid=(rows // block,),
        in_specs=[pl.BlockSpec((parts.shape[0], block, columns), lambda i: (0, i, 0))],
        out_specs=pl.BlockSpec((block, 2 * columns), lambda i: (i, 0)),
        compiler_params=pltpu.CompilerParams(vmem_limit_bytes=24 * 2**20),
        name="weight_total",
    )(parts)


def head_columns(weight):
    sides = jnp.swapaxes(weight, 0, 1)
    heads = sides.shape[2] // HD
    return jnp.concatenate(
        [sides[side, :, h * HD : (h + 1) * HD] for h in range(heads) for side in range(2)], axis=1
    )


def projection_kernel(which, context, weight, kv, total):
    step = pl.program_id(0)
    part = dot(context[...], head_columns(weight[...]), ((1,), (0,)))

    @pl.when(step == 0)
    def _():
        total[...] = part

    @pl.when(step > 0)
    def _():
        total[...] += part

    @pl.when(step == pl.num_programs(0) - 1)
    def _():
        kv[...] = total[...].astype(BF16)


def projection(which, context, weight):
    rows, width = context.shape
    columns = weight.shape[2] // 2
    depth = width // 3
    return pl.pallas_call(
        projection_kernel,
        out_shape=jax.ShapeDtypeStruct((rows, 2 * columns), BF16),
        grid_spec=pltpu.PrefetchScalarGridSpec(
            num_scalar_prefetch=1,
            grid=(width // depth,),
            in_specs=[
                pl.BlockSpec((rows, depth), lambda i, w: (0, i)),
                pl.BlockSpec((depth, 2, columns), lambda i, w: (i, 0, w[0])),
            ],
            out_specs=pl.BlockSpec((rows, 2 * columns), lambda i, w: (0, 0)),
            scratch_shapes=[pltpu.VMEM((rows, 2 * columns), F32)],
        ),
        compiler_params=pltpu.CompilerParams(vmem_limit_bytes=56 * 2**20),
        cost_estimate=pl.CostEstimate(
            flops=4 * rows * width * columns, bytes_accessed=20 * 2**20, transcendentals=0
        ),
        name="projection",
    )(which.reshape(1), context, weight)


def attention_kernel(meta, q_a, c_a, q_b, c_b, *refs):
    kv_refs, (od_a, od_b), g_refs = refs[:6], refs[6:8], refs[8:11]
    kv_s, q_s, c_s, g_s = refs[11:]
    rows, heads = q_a.shape[0], od_a.shape[1] // (2 * HD)
    member, side = meta[0], meta[6]
    scale = HD ** (-0.5)
    unit = scale * LOG2E
    results, terms = [], []
    near, far = 4 * side, 4 * (1 - side)
    order = (near + member, near + 1 - member, 2 + member, 3 - member, far + member, far + 1 - member)
    for ref, place in zip(kv_refs, order):
        kv_s[pl.ds(pl.multiple_of(place * rows, rows), rows), :] = ref[...]
    for ref, other, scratch in ((q_a, q_b, q_s), (c_a, c_b, c_s)):
        scratch[pl.ds(pl.multiple_of(member * rows, rows), rows), :] = ref[...]
        scratch[pl.ds(pl.multiple_of((1 - member) * rows, rows), rows), :] = other[...]
    span = 2 * REACH + 1
    block = lambda v, j: v[j * rows : (j + 1) * rows]
    products = []
    for i in range(PAIR):
        shard = slice(i * rows, (i + 1) * rows)
        window = slice(i * rows, (i + span) * rows)
        products.append(
            (
                dot(kv_s[window, :HD], q_s[shard, :], ((1,), (1,))),
                dot(kv_s[window, HD:], c_s[shard, :], ((1,), (1,))),
            )
        )
    for i in range(PAIR):
        window = slice(i * rows, (i + span) * rows)
        keys = kv_s[window, :HD]
        values = kv_s[window, HD:]
        low, high = meta[2 + 2 * i], meta[3 + 2 * i]
        scores, dprobs = products[i]
        offsets = []
        for j in range(span):
            shard = meta[1] + i + j
            offsets.append(jnp.where((shard >= low) & (shard <= high), 0.0, NEG_FILL))
        row_max = functools.reduce(
            jnp.maximum,
            [jnp.max(block(scores, j), axis=0, keepdims=True) + offsets[j] for j in range(span)],
        )
        expo = [
            jnp.exp2(block(scores, j) * unit + (offsets[j] - row_max * unit)) for j in range(span)
        ]
        norm = functools.reduce(jnp.add, [jnp.sum(e, axis=0, keepdims=True) for e in expo])
        probs = jnp.concatenate(expo, axis=0) * (1.0 / norm)
        rounded = probs.astype(BF16)
        delta = jnp.sum(dprobs * probs, axis=0, keepdims=True)
        dscores = (probs * (dprobs - delta)).astype(BF16)
        out = dot(values, rounded, ((0,), (0,)))
        dq = dot(keys, dscores, ((0,), (0,))) * scale
        terms.append((dscores, rounded))
        results.append([value.T.astype(BF16) for value in (out, dq)])
    head = pl.program_id(0)
    for part, (first, second) in enumerate(zip(*results)):
        columns = pl.ds(pl.multiple_of((part * heads + head) * HD, HD), HD)
        od_a[:, columns] = jnp.where(member == 0, first, second)
        od_b[:, columns] = jnp.where(member == 0, second, first)
    for w in range(WINDOW):
        users = [i for i in range(PAIR) if 0 <= w - i < span]
        over = slice(users[0] * rows, (users[-1] + 1) * rows)
        for part, (scratch, factor) in enumerate(((q_s, scale), (c_s, 1.0))):
            left = jnp.concatenate([block(terms[i][part], w - i) for i in users], axis=1)
            value = dot(left, scratch[over, :], ((1,), (0,)))
            value = value * factor if factor != 1.0 else value
            g_s[w * rows : (w + 1) * rows, part * HD : (part + 1) * HD] = value.astype(BF16)

    for index, place in enumerate(order):
        begin = index % PAIR * rows
        g_refs[index // PAIR][begin : begin + rows, :] = g_s[
            pl.ds(pl.multiple_of(place * rows, rows), rows), :
        ]


def attention(meta, qc_a, qc_b, kv_blocks):
    rows, half = kv_blocks[0].shape[0], qc_a.shape[1]
    heads = half // (2 * HD)
    one = lambda of: pl.BlockSpec((rows, HD), of)
    two = lambda of: pl.BlockSpec((rows, 2 * HD), of)
    plain = two(lambda h, m: (0, h))
    query, cot = one(lambda h, m: (0, h)), one(lambda h, m: (0, heads + h))
    shape = jax.ShapeDtypeStruct((rows, half), BF16)
    pair_shape = jax.ShapeDtypeStruct((PAIR * rows, half), BF16)
    whole = pl.BlockSpec((rows, half), lambda h, m: (0, 0))
    pair_block = pl.BlockSpec((PAIR * rows, 2 * HD), lambda h, m: (0, h))
    work = 2 * heads * rows * rows * 5
    return pl.pallas_call(
        attention_kernel,
        out_shape=[shape] * 2 + [pair_shape] * 3,
        grid_spec=pltpu.PrefetchScalarGridSpec(
            num_scalar_prefetch=1,
            grid=(heads,),
            in_specs=[query, cot, query, cot] + [plain] * 6,
            out_specs=[whole] * 2 + [pair_block] * 3,
            scratch_shapes=[
                pltpu.VMEM((WINDOW * rows, 2 * HD), BF16),
                pltpu.VMEM((PAIR * rows, HD), BF16),
                pltpu.VMEM((PAIR * rows, HD), BF16),
                pltpu.VMEM((WINDOW * rows, 2 * HD), BF16),
            ],
        ),
        compiler_params=pltpu.CompilerParams(vmem_limit_bytes=56 * 2**20),
        cost_estimate=pl.CostEstimate(
            flops=work * 10 * HD, bytes_accessed=8 * 2**20, transcendentals=work
        ),
        name="attention",
    )(meta, qc_a, qc_a, qc_b, qc_b, *kv_blocks)


def weight_kernel(own, own_z, pair, pair_z, grad, grad_z, out):
    rows = own.shape[0]
    total = dot(own[...], grad[:rows, :], ((0,), (0,)))
    total += dot(pair[...], grad[rows:, :], ((0,), (0,)))
    total += dot(own_z[...], grad_z[:rows, :], ((0,), (0,)))
    total += dot(pair_z[...], grad_z[rows:, :], ((0,), (0,)))
    out[...] = total.astype(BF16)


def weight_partial(contexts, grads):
    rows, width = contexts[0].shape
    columns = grads[0].shape[1]
    split = 4
    block = width // split
    return pl.pallas_call(
        weight_kernel,
        out_shape=jax.ShapeDtypeStruct((width, columns), BF16),
        grid=(split,),
        in_specs=[pl.BlockSpec((v.shape[0], block), lambda i: (0, i)) for v in contexts]
        + [pl.BlockSpec(g.shape, lambda i: (0, 0)) for g in grads],
        out_specs=pl.BlockSpec((block, columns), lambda i: (i, 0)),
        compiler_params=pltpu.CompilerParams(vmem_limit_bytes=24 * 2**20),
        cost_estimate=pl.CostEstimate(
            flops=8 * rows * width * columns, bytes_accessed=8 * 2**20, transcendentals=0
        ),
        name="weight_partial",
    )(*contexts, *grads)


def context_kernel(member, grad, grad_next, weight, out, both):
    half = grad.shape[1]

    @pl.when(pl.program_id(0) == 0)
    def _():
        both[:, pl.ds(pl.multiple_of(member[0] * half, half), half)] = grad[...]
        both[:, pl.ds(pl.multiple_of((1 - member[0]) * half, half), half)] = grad_next[...]

    out[...] = dot(both[...], head_columns(weight[...]), ((1,), (1,))).astype(BF16)


def context_partial(member, returned, other_rows, weight):
    rows, columns = other_rows.shape
    width = weight.shape[0]
    block = width // 4
    grad = pl.BlockSpec((rows, columns), lambda i, m: (0, 0))
    return pl.pallas_call(
        context_kernel,
        out_shape=jax.ShapeDtypeStruct((rows, width), BF16),
        grid_spec=pltpu.PrefetchScalarGridSpec(
            num_scalar_prefetch=1,
            grid=(width // block,),
            in_specs=[grad, grad, pl.BlockSpec((block, 2, columns), lambda i, m: (i, 0, 0))],
            out_specs=pl.BlockSpec((rows, block), lambda i, m: (0, i)),
            scratch_shapes=[pltpu.VMEM((rows, 2 * columns), BF16)],
        ),
        compiler_params=pltpu.CompilerParams(vmem_limit_bytes=50 * 2**20),
        cost_estimate=pl.CostEstimate(
            flops=4 * rows * width * columns, bytes_accessed=12 * 2**20, transcendentals=0
        ),
        name="context_partial",
    )(member.reshape(1), returned, other_rows, weight)


def local(queries, context, kv_weight, spans, cotangent):
    queries, context, cotangent = queries[0], context[0], cotangent[0]
    rows, columns = queries.shape
    heads = columns // HD
    width = context.shape[1]
    position = lax.axis_index("seq")
    member = position % PAIR
    side = position % XS // PAIR
    z = position // (XS * YS)
    same_x, cross_x, pair_x = in_row(2), in_row(3), in_row(1)
    half_of = lambda v, which: lax.dynamic_slice_in_dim(
        v, which * (v.shape[1] // 2), v.shape[1] // 2, axis=1
    )
    in_order = lambda mine, other: jnp.concatenate(
        [jnp.where(member == 0, mine, other), jnp.where(member == 0, other, mine)], axis=1
    )
    total = lambda parts: functools.reduce(jnp.add, [p.astype(F32) for p in parts])

    span_rows = jnp.broadcast_to(jnp.pad(spans[0].astype(BF16), ((0, 0), (0, columns - 2))), (16, columns))
    qc_of = lambda which: jnp.concatenate(
        [
            jnp.concatenate([half_of(queries, which), half_of(cotangent, which)], axis=1),
            span_rows,
        ],
        axis=0,
    )
    qc_a = moved(qc_of(member), "seq", same_x)
    qc_b = moved(qc_of(1 - member), "seq", cross_x)

    next_half = projection(1 - member, context, kv_weight[0])
    late_context, _ = lax.optimization_barrier((context, next_half))
    same_half = projection(member, late_context, kv_weight[0])
    same_half, qc_a, qc_b = lax.optimization_barrier((same_half, qc_a, qc_b))
    kv_blocks = [
        swapped(same_half, "tower"),
        moved_across(next_half, pair_x),
        moved_across(same_half, same_x),
        moved_across(next_half, cross_x),
        moved_across(same_half, next_row(False, 0)),
        moved_across(next_half, next_row(False, 1)),
    ]
    ctx_own = half_of(context, z)
    kv_blocks, late_own, ctx_rest = lax.optimization_barrier(
        (kv_blocks, ctx_own, half_of(context, 1 - z))
    )
    ctx_z = moved(ctx_rest, "seq", across_z())
    ctx_pair = moved(late_own, "seq", pair_x)

    span_a, span_b = qc_a[rows, :2].astype(jnp.int32), qc_b[rows, :2].astype(jnp.int32)
    first = jnp.where(member == 0, span_a, span_b)
    second = jnp.where(member == 0, span_b, span_a)
    base = position - member - 4 * side
    meta = jnp.concatenate([jnp.stack([member, base]), first, second, side[None]]).astype(jnp.int32)
    od_a, od_b, g_near, g_mid, g_far = attention(meta, qc_a, qc_b, kv_blocks)

    g_mid = moved_across(g_mid, same_x)
    g_near, ctx_pair, ctx_z = lax.optimization_barrier((g_near, ctx_pair, ctx_z))
    g_far = moved_across(g_far, next_row(True, 0))
    returned = total([swapped(g_near, "tower"), g_mid, g_far]).astype(BF16)
    late_z, _ = lax.optimization_barrier((ctx_z, returned))
    ctx_pair_z = moved(late_z, "seq", pair_x)
    returned_z = moved(returned, "seq", across_z())
    other_rows = moved(returned[rows:], "seq", pair_x)
    od_b, _ = lax.optimization_barrier((od_b, returned))
    od_b = moved(od_b, "seq", cross_x)
    other_rows, od_b = lax.optimization_barrier((other_rows, od_b))
    partial_ctx = context_partial(member, returned, other_rows, kv_weight[0])
    od_a, _ = lax.optimization_barrier((od_a, partial_ctx))
    od_a = moved(od_a, "seq", same_x)
    sum_parts = [partial_ctx[:, : width // 3], partial_ctx[:, width // 3 :]]
    sum_first = swapped(sum_parts[0], "mp")


    partial_w = weight_partial([ctx_own, ctx_z, ctx_pair, ctx_pair_z], [returned, returned_z])
    partial_w, sum_first, od_a = lax.optimization_barrier((partial_w, sum_first, od_a))
    late_half, _ = lax.optimization_barrier((sum_parts[1], sum_first))
    sum_second = swapped(late_half, "mp")
    plane = YS * XS
    groups = [[z_ * plane + i for i in range(plane)] for z_ in range(ZS)]
    parts = lax.all_to_all(
        partial_w.reshape(plane, -1, columns), "seq", 0, 0, axis_index_groups=groups
    )
    weight_grad = weight_total(parts).reshape(-1, 2, columns)[None]

    context_grad = jnp.concatenate(
        [
            total([mine, other]).astype(BF16)
            for mine, other in zip(sum_parts, (sum_first, sum_second))
        ],
        axis=1,
    )
    attn_out = in_order(od_a[:, : columns // 2], od_b[:, : columns // 2])
    query_grad = in_order(od_a[:, columns // 2 :], od_b[:, columns // 2 :])
    return attn_out[None], query_grad[None], context_grad[None], weight_grad


def solution(mesh):
    return jax.shard_map(
        local,
        mesh=mesh,
        in_specs=(
            P("tower", "seq", "mp"),
            P("tower", "seq", None),
            P("tower", None, None, "mp"),
            P("tower", "seq", None),
            P("tower", "seq", "mp"),
        ),
        out_specs=(
            P("tower", "seq", "mp"),
            P("tower", "seq", "mp"),
            P("tower", "seq", None),
            P("tower", "seq", None, "mp"),
        ),
        check_vma=False,
    )
```

```python
import functools

import jax
import jax.numpy as jnp
from jax import lax
from jax.experimental import pallas as pl
from jax.experimental.pallas import tpu as pltpu
from jax.sharding import PartitionSpec as P

HD = 128
REACH = 2
NEG_FILL = -1e30
LOG2E = 1.4426950408889634
F32, BF16 = jnp.float32, jnp.bfloat16
ZS, YS, XS = 2, 4, 4
PAIR = 2
WINDOW = 6


def moved(value, axis, pairs):
    return lax.ppermute(value, axis, pairs)


def swapped(value, axis):
    return moved(value, axis, [(0, 1), (1, 0)])


def moved_across(value, pairs):
    both = [
        (tower * ZS * YS * XS + source, (1 - tower) * ZS * YS * XS + target)
        for tower in range(2)
        for source, target in pairs
    ]
    return lax.ppermute(value, ("tower", "seq"), both)


def seq_pairs(to):
    pairs = []
    for source in range(ZS * YS * XS):
        row, x = to(source // XS, source % XS)
        if 0 <= row < ZS * YS:
            pairs.append((source, row * XS + x))
    return pairs


def across_z():
    return seq_pairs(lambda row, x: ((row + YS) % (ZS * YS), x))


def in_row(flip):
    return seq_pairs(lambda row, x: (row, x ^ flip))


def next_row(back, flip):
    return seq_pairs(lambda row, x: (row + (1 if (x >= PAIR) != back else -1), x ^ flip))


def dot(a, b, dims):
    return lax.dot_general(a, b, ((dims[0], dims[1]), ((), ())), preferred_element_type=F32)


def total_kernel(parts, out):
    columns = parts.shape[2]
    heads = columns // (2 * HD)
    for half in range(PAIR):
        total = parts[half].astype(F32)
        for source in range(half + PAIR, parts.shape[0], PAIR):
            total += parts[source].astype(F32)
        for h in range(heads):
            for side in range(2):
                begin = (2 * h + side) * HD
                place = side * columns + (half * heads + h) * HD
                out[:, place : place + HD] = total[:, begin : begin + HD].astype(BF16)


def weight_total(parts):
    rows, columns = parts.shape[1:]
    block = rows // 2
    return pl.pallas_call(
        total_kernel,
        out_shape=jax.ShapeDtypeStruct((rows, 2 * columns), BF16),
        grid=(rows // block,),
        in_specs=[pl.BlockSpec((parts.shape[0], block, columns), lambda i: (0, i, 0))],
        out_specs=pl.BlockSpec((block, 2 * columns), lambda i: (i, 0)),
        compiler_params=pltpu.CompilerParams(vmem_limit_bytes=24 * 2**20),
        name="weight_total",
    )(parts)


def head_columns(weight):
    sides = jnp.swapaxes(weight, 0, 1)
    heads = sides.shape[2] // HD
    return jnp.concatenate(
        [sides[side, :, h * HD : (h + 1) * HD] for h in range(heads) for side in range(2)], axis=1
    )


def projection_kernel(which, context, weight, kv, total):
    step = pl.program_id(0)
    part = dot(context[...], head_columns(weight[...]), ((1,), (0,)))

    @pl.when(step == 0)
    def _():
        total[...] = part

    @pl.when(step > 0)
    def _():
        total[...] += part

    @pl.when(step == pl.num_programs(0) - 1)
    def _():
        kv[...] = total[...].astype(BF16)


def projection(which, context, weight):
    rows, width = context.shape
    columns = weight.shape[2] // 2
    depth = width // 3
    return pl.pallas_call(
        projection_kernel,
        out_shape=jax.ShapeDtypeStruct((rows, 2 * columns), BF16),
        grid_spec=pltpu.PrefetchScalarGridSpec(
            num_scalar_prefetch=1,
            grid=(width // depth,),
            in_specs=[
                pl.BlockSpec((rows, depth), lambda i, w: (0, i)),
                pl.BlockSpec((depth, 2, columns), lambda i, w: (i, 0, w[0])),
            ],
            out_specs=pl.BlockSpec((rows, 2 * columns), lambda i, w: (0, 0)),
            scratch_shapes=[pltpu.VMEM((rows, 2 * columns), F32)],
        ),
        compiler_params=pltpu.CompilerParams(vmem_limit_bytes=56 * 2**20),
        cost_estimate=pl.CostEstimate(
            flops=4 * rows * width * columns, bytes_accessed=20 * 2**20, transcendentals=0
        ),
        name="projection",
    )(which.reshape(1), context, weight)


def attention_kernel(meta, q_a, c_a, q_b, c_b, *refs):
    kv_refs, (od_a, od_b), g_refs = refs[:6], refs[6:8], refs[8:11]
    kv_s, q_s, c_s, g_s = refs[11:]
    rows, heads = q_a.shape[0], od_a.shape[1] // (2 * HD)
    member, side = meta[0], meta[6]
    scale = HD ** (-0.5)
    unit = scale * LOG2E
    results, terms = [], []
    near, far = 4 * side, 4 * (1 - side)
    order = (near + member, near + 1 - member, 2 + member, 3 - member, far + member, far + 1 - member)
    for ref, place in zip(kv_refs, order):
        kv_s[pl.ds(pl.multiple_of(place * rows, rows), rows), :] = ref[...]
    for ref, other, scratch in ((q_a, q_b, q_s), (c_a, c_b, c_s)):
        scratch[pl.ds(pl.multiple_of(member * rows, rows), rows), :] = ref[...]
        scratch[pl.ds(pl.multiple_of((1 - member) * rows, rows), rows), :] = other[...]
    span = 2 * REACH + 1
    block = lambda v, j: v[j * rows : (j + 1) * rows]
    products, halves = [], []
    for i in range(PAIR):
        shard = slice(i * rows, (i + 1) * rows)
        window = slice(i * rows, (i + span) * rows)
        products.append(
            (
                dot(kv_s[window, :HD], q_s[shard, :], ((1,), (1,))),
                dot(kv_s[window, HD:], c_s[shard, :], ((1,), (1,))),
            )
        )
    for i in range(PAIR):
        window = slice(i * rows, (i + span) * rows)
        keys = kv_s[window, :HD]
        values = kv_s[window, HD:]
        low, high = meta[2 + 2 * i], meta[3 + 2 * i]
        scores, dprobs = products[i]
        offsets = []
        for j in range(span):
            shard = meta[1] + i + j
            offsets.append(jnp.where((shard >= low) & (shard <= high), 0.0, NEG_FILL))
        row_max = functools.reduce(
            jnp.maximum,
            [jnp.max(block(scores, j), axis=0, keepdims=True) + offsets[j] for j in range(span)],
        )
        expo = [
            jnp.exp2(block(scores, j) * unit + (offsets[j] - row_max * unit)) for j in range(span)
        ]
        norm = functools.reduce(jnp.add, [jnp.sum(e, axis=0, keepdims=True) for e in expo])
        probs = jnp.concatenate(expo, axis=0) * (1.0 / norm)
        rounded = probs.astype(BF16)
        delta = jnp.sum(dprobs * probs, axis=0, keepdims=True)
        out = dot(values, rounded, ((0,), (0,)))
        halves.append((keys, probs, rounded, dprobs, delta, out))
    for keys, probs, rounded, dprobs, delta, out in halves:
        dscores = (probs * (dprobs - delta)).astype(BF16)
        dq = dot(keys, dscores, ((0,), (0,))) * scale
        terms.append((dscores, rounded))
        results.append([value.T.astype(BF16) for value in (out, dq)])
    head = pl.program_id(0)
    for part, (first, second) in enumerate(zip(*results)):
        columns = pl.ds(pl.multiple_of((part * heads + head) * HD, HD), HD)
        od_a[:, columns] = jnp.where(member == 0, first, second)
        od_b[:, columns] = jnp.where(member == 0, second, first)
    for w in range(WINDOW):
        users = [i for i in range(PAIR) if 0 <= w - i < span]
        over = slice(users[0] * rows, (users[-1] + 1) * rows)
        for part, (scratch, factor) in enumerate(((q_s, scale), (c_s, 1.0))):
            left = jnp.concatenate([block(terms[i][part], w - i) for i in users], axis=1)
            value = dot(left, scratch[over, :], ((1,), (0,)))
            value = value * factor if factor != 1.0 else value
            g_s[w * rows : (w + 1) * rows, part * HD : (part + 1) * HD] = value.astype(BF16)

    for index, place in enumerate(order):
        begin = index % PAIR * rows
        g_refs[index // PAIR][begin : begin + rows, :] = g_s[
            pl.ds(pl.multiple_of(place * rows, rows), rows), :
        ]


def attention(meta, qc_a, qc_b, kv_blocks):
    rows, half = kv_blocks[0].shape[0], qc_a.shape[1]
    heads = half // (2 * HD)
    one = lambda of: pl.BlockSpec((rows, HD), of)
    two = lambda of: pl.BlockSpec((rows, 2 * HD), of)
    plain = two(lambda h, m: (0, h))
    query, cot = one(lambda h, m: (0, h)), one(lambda h, m: (0, heads + h))
    shape = jax.ShapeDtypeStruct((rows, half), BF16)
    pair_shape = jax.ShapeDtypeStruct((PAIR * rows, half), BF16)
    whole = pl.BlockSpec((rows, half), lambda h, m: (0, 0))
    pair_block = pl.BlockSpec((PAIR * rows, 2 * HD), lambda h, m: (0, h))
    work = 2 * heads * rows * rows * 5
    return pl.pallas_call(
        attention_kernel,
        out_shape=[shape] * 2 + [pair_shape] * 3,
        grid_spec=pltpu.PrefetchScalarGridSpec(
            num_scalar_prefetch=1,
            grid=(heads,),
            in_specs=[query, cot, query, cot] + [plain] * 6,
            out_specs=[whole] * 2 + [pair_block] * 3,
            scratch_shapes=[
                pltpu.VMEM((WINDOW * rows, 2 * HD), BF16),
                pltpu.VMEM((PAIR * rows, HD), BF16),
                pltpu.VMEM((PAIR * rows, HD), BF16),
                pltpu.VMEM((WINDOW * rows, 2 * HD), BF16),
            ],
        ),
        compiler_params=pltpu.CompilerParams(vmem_limit_bytes=56 * 2**20),
        cost_estimate=pl.CostEstimate(
            flops=work * 10 * HD, bytes_accessed=8 * 2**20, transcendentals=work
        ),
        name="attention",
    )(meta, qc_a, qc_a, qc_b, qc_b, *kv_blocks)


def weight_kernel(own, own_z, pair, pair_z, grad, grad_z, out):
    rows = own.shape[0]
    total = dot(own[...], grad[:rows, :], ((0,), (0,)))
    total += dot(pair[...], grad[rows:, :], ((0,), (0,)))
    total += dot(own_z[...], grad_z[:rows, :], ((0,), (0,)))
    total += dot(pair_z[...], grad_z[rows:, :], ((0,), (0,)))
    out[...] = total.astype(BF16)


def weight_partial(contexts, grads):
    rows, width = contexts[0].shape
    columns = grads[0].shape[1]
    split = 4
    block = width // split
    return pl.pallas_call(
        weight_kernel,
        out_shape=jax.ShapeDtypeStruct((width, columns), BF16),
        grid=(split,),
        in_specs=[pl.BlockSpec((v.shape[0], block), lambda i: (0, i)) for v in contexts]
        + [pl.BlockSpec(g.shape, lambda i: (0, 0)) for g in grads],
        out_specs=pl.BlockSpec((block, columns), lambda i: (i, 0)),
        compiler_params=pltpu.CompilerParams(vmem_limit_bytes=24 * 2**20),
        cost_estimate=pl.CostEstimate(
            flops=8 * rows * width * columns, bytes_accessed=8 * 2**20, transcendentals=0
        ),
        name="weight_partial",
    )(*contexts, *grads)


def context_kernel(member, grad, grad_next, weight, out, both):
    half = grad.shape[1]

    @pl.when(pl.program_id(0) == 0)
    def _():
        both[:, pl.ds(pl.multiple_of(member[0] * half, half), half)] = grad[...]
        both[:, pl.ds(pl.multiple_of((1 - member[0]) * half, half), half)] = grad_next[...]

    out[...] = dot(both[...], head_columns(weight[...]), ((1,), (1,))).astype(BF16)


def context_partial(member, returned, other_rows, weight):
    rows, columns = other_rows.shape
    width = weight.shape[0]
    block = width // 4
    grad = pl.BlockSpec((rows, columns), lambda i, m: (0, 0))
    return pl.pallas_call(
        context_kernel,
        out_shape=jax.ShapeDtypeStruct((rows, width), BF16),
        grid_spec=pltpu.PrefetchScalarGridSpec(
            num_scalar_prefetch=1,
            grid=(width // block,),
            in_specs=[grad, grad, pl.BlockSpec((block, 2, columns), lambda i, m: (i, 0, 0))],
            out_specs=pl.BlockSpec((rows, block), lambda i, m: (0, i)),
            scratch_shapes=[pltpu.VMEM((rows, 2 * columns), BF16)],
        ),
        compiler_params=pltpu.CompilerParams(vmem_limit_bytes=50 * 2**20),
        cost_estimate=pl.CostEstimate(
            flops=4 * rows * width * columns, bytes_accessed=12 * 2**20, transcendentals=0
        ),
        name="context_partial",
    )(member.reshape(1), returned, other_rows, weight)


def local(queries, context, kv_weight, spans, cotangent):
    queries, context, cotangent = queries[0], context[0], cotangent[0]
    rows, columns = queries.shape
    heads = columns // HD
    width = context.shape[1]
    position = lax.axis_index("seq")
    member = position % PAIR
    side = position % XS // PAIR
    z = position // (XS * YS)
    same_x, cross_x, pair_x = in_row(2), in_row(3), in_row(1)
    half_of = lambda v, which: lax.dynamic_slice_in_dim(
        v, which * (v.shape[1] // 2), v.shape[1] // 2, axis=1
    )
    in_order = lambda mine, other: jnp.concatenate(
        [jnp.where(member == 0, mine, other), jnp.where(member == 0, other, mine)], axis=1
    )
    total = lambda parts: functools.reduce(jnp.add, [p.astype(F32) for p in parts])

    span_rows = jnp.broadcast_to(jnp.pad(spans[0].astype(BF16), ((0, 0), (0, columns - 2))), (16, columns))
    qc_of = lambda which: jnp.concatenate(
        [
            jnp.concatenate([half_of(queries, which), half_of(cotangent, which)], axis=1),
            span_rows,
        ],
        axis=0,
    )
    qc_a = moved(qc_of(member), "seq", same_x)
    qc_b = moved(qc_of(1 - member), "seq", cross_x)

    next_half = projection(1 - member, context, kv_weight[0])
    late_context, _ = lax.optimization_barrier((context, next_half))
    same_half = projection(member, late_context, kv_weight[0])
    same_half, qc_a, qc_b = lax.optimization_barrier((same_half, qc_a, qc_b))
    kv_blocks = [
        swapped(same_half, "tower"),
        moved_across(next_half, pair_x),
        moved_across(same_half, same_x),
        moved_across(next_half, cross_x),
        moved_across(same_half, next_row(False, 0)),
        moved_across(next_half, next_row(False, 1)),
    ]
    ctx_own = half_of(context, z)
    kv_blocks, late_own, ctx_rest = lax.optimization_barrier(
        (kv_blocks, ctx_own, half_of(context, 1 - z))
    )
    ctx_z = moved(ctx_rest, "seq", across_z())
    ctx_pair = moved(late_own, "seq", pair_x)

    span_a, span_b = qc_a[rows, :2].astype(jnp.int32), qc_b[rows, :2].astype(jnp.int32)
    first = jnp.where(member == 0, span_a, span_b)
    second = jnp.where(member == 0, span_b, span_a)
    base = position - member - 4 * side
    meta = jnp.concatenate([jnp.stack([member, base]), first, second, side[None]]).astype(jnp.int32)
    od_a, od_b, g_near, g_mid, g_far = attention(meta, qc_a, qc_b, kv_blocks)

    g_mid = moved_across(g_mid, same_x)
    g_near, ctx_pair, ctx_z = lax.optimization_barrier((g_near, ctx_pair, ctx_z))
    g_far = moved_across(g_far, next_row(True, 0))
    returned = total([swapped(g_near, "tower"), g_mid, g_far]).astype(BF16)
    late_z, _ = lax.optimization_barrier((ctx_z, returned))
    ctx_pair_z = moved(late_z, "seq", pair_x)
    returned_z = moved(returned, "seq", across_z())
    other_rows = moved(returned[rows:], "seq", pair_x)
    od_b, _ = lax.optimization_barrier((od_b, returned))
    od_b = moved(od_b, "seq", cross_x)
    other_rows, od_b = lax.optimization_barrier((other_rows, od_b))
    partial_ctx = context_partial(member, returned, other_rows, kv_weight[0])
    od_a, _ = lax.optimization_barrier((od_a, partial_ctx))
    od_a = moved(od_a, "seq", same_x)
    sum_parts = [partial_ctx[:, : width // 3], partial_ctx[:, width // 3 :]]
    sum_first = swapped(sum_parts[0], "mp")


    partial_w = weight_partial([ctx_own, ctx_z, ctx_pair, ctx_pair_z], [returned, returned_z])
    partial_w, sum_first, od_a = lax.optimization_barrier((partial_w, sum_first, od_a))
    late_half, _ = lax.optimization_barrier((sum_parts[1], sum_first))
    sum_second = swapped(late_half, "mp")
    plane = YS * XS
    groups = [[z_ * plane + i for i in range(plane)] for z_ in range(ZS)]
    parts = lax.all_to_all(
        partial_w.reshape(plane, -1, columns), "seq", 0, 0, axis_index_groups=groups
    )
    weight_grad = weight_total(parts).reshape(-1, 2, columns)[None]

    context_grad = jnp.concatenate(
        [
            total([mine, other]).astype(BF16)
            for mine, other in zip(sum_parts, (sum_first, sum_second))
        ],
        axis=1,
    )
    attn_out = in_order(od_a[:, : columns // 2], od_b[:, : columns // 2])
    query_grad = in_order(od_a[:, columns // 2 :], od_b[:, columns // 2 :])
    return attn_out[None], query_grad[None], context_grad[None], weight_grad


def solution(mesh):
    return jax.shard_map(
        local,
        mesh=mesh,
        in_specs=(
            P("tower", "seq", "mp"),
            P("tower", "seq", None),
            P("tower", None, None, "mp"),
            P("tower", "seq", None),
            P("tower", "seq", "mp"),
        ),
        out_specs=(
            P("tower", "seq", "mp"),
            P("tower", "seq", "mp"),
            P("tower", "seq", None),
            P("tower", "seq", None, "mp"),
        ),
        check_vma=False,
    )
```

```python
import functools

import jax
import jax.numpy as jnp
from jax import lax
from jax.experimental import pallas as pl
from jax.experimental.pallas import tpu as pltpu
from jax.sharding import PartitionSpec as P

HD = 128
REACH = 2
NEG_FILL = -1e30
LOG2E = 1.4426950408889634
F32, BF16 = jnp.float32, jnp.bfloat16
ZS, YS, XS = 2, 4, 4
PAIR = 2
WINDOW = 6


def moved(value, axis, pairs):
    return lax.ppermute(value, axis, pairs)


def swapped(value, axis):
    return moved(value, axis, [(0, 1), (1, 0)])


def moved_across(value, pairs):
    both = [
        (tower * ZS * YS * XS + source, (1 - tower) * ZS * YS * XS + target)
        for tower in range(2)
        for source, target in pairs
    ]
    return lax.ppermute(value, ("tower", "seq"), both)


def seq_pairs(to):
    pairs = []
    for source in range(ZS * YS * XS):
        row, x = to(source // XS, source % XS)
        if 0 <= row < ZS * YS:
            pairs.append((source, row * XS + x))
    return pairs


def across_z():
    return seq_pairs(lambda row, x: ((row + YS) % (ZS * YS), x))


def in_row(flip):
    return seq_pairs(lambda row, x: (row, x ^ flip))


def next_row(back, flip):
    return seq_pairs(lambda row, x: (row + (1 if (x >= PAIR) != back else -1), x ^ flip))


def dot(a, b, dims):
    return lax.dot_general(a, b, ((dims[0], dims[1]), ((), ())), preferred_element_type=F32)


def total_kernel(parts, out):
    columns = parts.shape[2]
    heads = columns // (2 * HD)
    sides = ([], [])
    for half in range(PAIR):
        total = parts[half].astype(F32)
        for source in range(half + PAIR, parts.shape[0], PAIR):
            total += parts[source].astype(F32)
        for h in range(heads):
            for side in range(2):
                begin = (2 * h + side) * HD
                sides[side].append(total[:, begin : begin + HD].astype(BF16))
    both = jnp.stack([jnp.concatenate(side, axis=1) for side in sides], axis=0)
    out[...] = jnp.swapaxes(both, 0, 1)


def weight_total(parts):
    rows, columns = parts.shape[1:]
    block = rows // 2
    return pl.pallas_call(
        total_kernel,
        out_shape=jax.ShapeDtypeStruct((rows, 2, columns), BF16),
        grid=(rows // block,),
        in_specs=[pl.BlockSpec((parts.shape[0], block, columns), lambda i: (0, i, 0))],
        out_specs=pl.BlockSpec((block, 2, columns), lambda i: (i, 0, 0)),
        compiler_params=pltpu.CompilerParams(vmem_limit_bytes=24 * 2**20),
        name="weight_total",
    )(parts)


def head_columns(weight):
    sides = jnp.swapaxes(weight, 0, 1)
    heads = sides.shape[2] // HD
    return jnp.concatenate(
        [sides[side, :, h * HD : (h + 1) * HD] for h in range(heads) for side in range(2)], axis=1
    )


def projection_kernel(which, context, weight, kv, total):
    step = pl.program_id(0)
    part = dot(context[...], head_columns(weight[...]), ((1,), (0,)))

    @pl.when(step == 0)
    def _():
        total[...] = part

    @pl.when(step > 0)
    def _():
        total[...] += part

    @pl.when(step == pl.num_programs(0) - 1)
    def _():
        kv[...] = total[...].astype(BF16)


def projection(which, context, weight):
    rows, width = context.shape
    columns = weight.shape[2] // 2
    depth = width // 3
    return pl.pallas_call(
        projection_kernel,
        out_shape=jax.ShapeDtypeStruct((rows, 2 * columns), BF16),
        grid_spec=pltpu.PrefetchScalarGridSpec(
            num_scalar_prefetch=1,
            grid=(width // depth,),
            in_specs=[
                pl.BlockSpec((rows, depth), lambda i, w: (0, i)),
                pl.BlockSpec((depth, 2, columns), lambda i, w: (i, 0, w[0])),
            ],
            out_specs=pl.BlockSpec((rows, 2 * columns), lambda i, w: (0, 0)),
            scratch_shapes=[pltpu.VMEM((rows, 2 * columns), F32)],
        ),
        compiler_params=pltpu.CompilerParams(vmem_limit_bytes=56 * 2**20),
        cost_estimate=pl.CostEstimate(
            flops=4 * rows * width * columns, bytes_accessed=20 * 2**20, transcendentals=0
        ),
        name="projection",
    )(which.reshape(1), context, weight)


def attention_kernel(meta, q_a, c_a, q_b, c_b, *refs):
    kv_refs, (od_a, od_b), g_refs = refs[:6], refs[6:8], refs[8:11]
    kv_s, q_s, c_s, g_s = refs[11:]
    rows, heads = q_a.shape[0], od_a.shape[1] // (2 * HD)
    member, side = meta[0], meta[6]
    scale = HD ** (-0.5)
    unit = scale * LOG2E
    results, terms = [], []
    near, far = 4 * side, 4 * (1 - side)
    order = (near + member, near + 1 - member, 2 + member, 3 - member, far + member, far + 1 - member)
    for ref, place in zip(kv_refs, order):
        kv_s[pl.ds(pl.multiple_of(place * rows, rows), rows), :] = ref[...]
    for ref, other, scratch in ((q_a, q_b, q_s), (c_a, c_b, c_s)):
        scratch[pl.ds(pl.multiple_of(member * rows, rows), rows), :] = ref[...]
        scratch[pl.ds(pl.multiple_of((1 - member) * rows, rows), rows), :] = other[...]
    span = 2 * REACH + 1
    block = lambda v, j: v[j * rows : (j + 1) * rows]
    products, halves = [], []
    for i in range(PAIR):
        shard = slice(i * rows, (i + 1) * rows)
        window = slice(i * rows, (i + span) * rows)
        products.append(
            (
                dot(kv_s[window, :HD], q_s[shard, :], ((1,), (1,))),
                dot(kv_s[window, HD:], c_s[shard, :], ((1,), (1,))),
            )
        )
    for i in range(PAIR):
        window = slice(i * rows, (i + span) * rows)
        keys = kv_s[window, :HD]
        values = kv_s[window, HD:]
        low, high = meta[2 + 2 * i], meta[3 + 2 * i]
        scores, dprobs = products[i]
        offsets = []
        for j in range(span):
            shard = meta[1] + i + j
            offsets.append(jnp.where((shard >= low) & (shard <= high), 0.0, NEG_FILL))
        row_max = functools.reduce(
            jnp.maximum,
            [jnp.max(block(scores, j), axis=0, keepdims=True) + offsets[j] for j in range(span)],
        )
        expo = [
            jnp.exp2(block(scores, j) * unit + (offsets[j] - row_max * unit)) for j in range(span)
        ]
        norm = functools.reduce(jnp.add, [jnp.sum(e, axis=0, keepdims=True) for e in expo])
        probs = jnp.concatenate(expo, axis=0) * (1.0 / norm)
        rounded = probs.astype(BF16)
        delta = jnp.sum(dprobs * probs, axis=0, keepdims=True)
        out = dot(values, rounded, ((0,), (0,)))
        halves.append((keys, probs, rounded, dprobs, delta, out))
    for keys, probs, rounded, dprobs, delta, out in halves:
        dscores = (probs * (dprobs - delta)).astype(BF16)
        dq = dot(keys, dscores, ((0,), (0,))) * scale
        terms.append((dscores, rounded))
        results.append([value.T.astype(BF16) for value in (out, dq)])
    head = pl.program_id(0)
    for part, (first, second) in enumerate(zip(*results)):
        columns = pl.ds(pl.multiple_of((part * heads + head) * HD, HD), HD)
        od_a[:, columns] = jnp.where(member == 0, first, second)
        od_b[:, columns] = jnp.where(member == 0, second, first)
    for w in range(WINDOW):
        users = [i for i in range(PAIR) if 0 <= w - i < span]
        over = slice(users[0] * rows, (users[-1] + 1) * rows)
        for part, (scratch, factor) in enumerate(((q_s, scale), (c_s, 1.0))):
            left = jnp.concatenate([block(terms[i][part], w - i) for i in users], axis=1)
            value = dot(left, scratch[over, :], ((1,), (0,)))
            value = value * factor if factor != 1.0 else value
            g_s[w * rows : (w + 1) * rows, part * HD : (part + 1) * HD] = value.astype(BF16)

    for index, place in enumerate(order):
        begin = index % PAIR * rows
        g_refs[index // PAIR][begin : begin + rows, :] = g_s[
            pl.ds(pl.multiple_of(place * rows, rows), rows), :
        ]


def attention(meta, qc_a, qc_b, kv_blocks):
    rows, half = kv_blocks[0].shape[0], qc_a.shape[1]
    heads = half // (2 * HD)
    one = lambda of: pl.BlockSpec((rows, HD), of)
    two = lambda of: pl.BlockSpec((rows, 2 * HD), of)
    plain = two(lambda h, m: (0, h))
    query, cot = one(lambda h, m: (0, h)), one(lambda h, m: (0, heads + h))
    shape = jax.ShapeDtypeStruct((rows, half), BF16)
    pair_shape = jax.ShapeDtypeStruct((PAIR * rows, half), BF16)
    whole = pl.BlockSpec((rows, half), lambda h, m: (0, 0))
    pair_block = pl.BlockSpec((PAIR * rows, 2 * HD), lambda h, m: (0, h))
    work = 2 * heads * rows * rows * 5
    return pl.pallas_call(
        attention_kernel,
        out_shape=[shape] * 2 + [pair_shape] * 3,
        grid_spec=pltpu.PrefetchScalarGridSpec(
            num_scalar_prefetch=1,
            grid=(heads,),
            in_specs=[query, cot, query, cot] + [plain] * 6,
            out_specs=[whole] * 2 + [pair_block] * 3,
            scratch_shapes=[
                pltpu.VMEM((WINDOW * rows, 2 * HD), BF16),
                pltpu.VMEM((PAIR * rows, HD), BF16),
                pltpu.VMEM((PAIR * rows, HD), BF16),
                pltpu.VMEM((WINDOW * rows, 2 * HD), BF16),
            ],
        ),
        compiler_params=pltpu.CompilerParams(vmem_limit_bytes=56 * 2**20),
        cost_estimate=pl.CostEstimate(
            flops=work * 10 * HD, bytes_accessed=8 * 2**20, transcendentals=work
        ),
        name="attention",
    )(meta, qc_a, qc_a, qc_b, qc_b, *kv_blocks)


def weight_kernel(own, own_z, pair, pair_z, grad, grad_z, out):
    rows = own.shape[0]
    total = dot(own[...], grad[:rows, :], ((0,), (0,)))
    total += dot(pair[...], grad[rows:, :], ((0,), (0,)))
    total += dot(own_z[...], grad_z[:rows, :], ((0,), (0,)))
    total += dot(pair_z[...], grad_z[rows:, :], ((0,), (0,)))
    out[...] = total.astype(BF16)


def weight_partial(contexts, grads):
    rows, width = contexts[0].shape
    columns = grads[0].shape[1]
    split = 4
    block = width // split
    return pl.pallas_call(
        weight_kernel,
        out_shape=jax.ShapeDtypeStruct((width, columns), BF16),
        grid=(split,),
        in_specs=[pl.BlockSpec((v.shape[0], block), lambda i: (0, i)) for v in contexts]
        + [pl.BlockSpec(g.shape, lambda i: (0, 0)) for g in grads],
        out_specs=pl.BlockSpec((block, columns), lambda i: (i, 0)),
        compiler_params=pltpu.CompilerParams(vmem_limit_bytes=24 * 2**20),
        cost_estimate=pl.CostEstimate(
            flops=8 * rows * width * columns, bytes_accessed=8 * 2**20, transcendentals=0
        ),
        name="weight_partial",
    )(*contexts, *grads)


def context_kernel(member, grad, grad_next, weight, out, both):
    half = grad.shape[1]

    @pl.when(pl.program_id(0) == 0)
    def _():
        both[:, pl.ds(pl.multiple_of(member[0] * half, half), half)] = grad[...]
        both[:, pl.ds(pl.multiple_of((1 - member[0]) * half, half), half)] = grad_next[...]

    out[...] = dot(both[...], head_columns(weight[...]), ((1,), (1,))).astype(BF16)


def context_partial(member, returned, other_rows, weight):
    rows, columns = other_rows.shape
    width = weight.shape[0]
    block = width // 4
    grad = pl.BlockSpec((rows, columns), lambda i, m: (0, 0))
    return pl.pallas_call(
        context_kernel,
        out_shape=jax.ShapeDtypeStruct((rows, width), BF16),
        grid_spec=pltpu.PrefetchScalarGridSpec(
            num_scalar_prefetch=1,
            grid=(width // block,),
            in_specs=[grad, grad, pl.BlockSpec((block, 2, columns), lambda i, m: (i, 0, 0))],
            out_specs=pl.BlockSpec((rows, block), lambda i, m: (0, i)),
            scratch_shapes=[pltpu.VMEM((rows, 2 * columns), BF16)],
        ),
        compiler_params=pltpu.CompilerParams(vmem_limit_bytes=50 * 2**20),
        cost_estimate=pl.CostEstimate(
            flops=4 * rows * width * columns, bytes_accessed=12 * 2**20, transcendentals=0
        ),
        name="context_partial",
    )(member.reshape(1), returned, other_rows, weight)


def local(queries, context, kv_weight, spans, cotangent):
    queries, context, cotangent = queries[0], context[0], cotangent[0]
    rows, columns = queries.shape
    heads = columns // HD
    width = context.shape[1]
    position = lax.axis_index("seq")
    member = position % PAIR
    side = position % XS // PAIR
    z = position // (XS * YS)
    same_x, cross_x, pair_x = in_row(2), in_row(3), in_row(1)
    half_of = lambda v, which: lax.dynamic_slice_in_dim(
        v, which * (v.shape[1] // 2), v.shape[1] // 2, axis=1
    )
    in_order = lambda mine, other: jnp.concatenate(
        [jnp.where(member == 0, mine, other), jnp.where(member == 0, other, mine)], axis=1
    )
    total = lambda parts: functools.reduce(jnp.add, [p.astype(F32) for p in parts])

    span_rows = jnp.broadcast_to(jnp.pad(spans[0].astype(BF16), ((0, 0), (0, columns - 2))), (16, columns))
    qc_of = lambda which: jnp.concatenate(
        [
            jnp.concatenate([half_of(queries, which), half_of(cotangent, which)], axis=1),
            span_rows,
        ],
        axis=0,
    )
    qc_a = moved(qc_of(member), "seq", same_x)
    qc_b = moved(qc_of(1 - member), "seq", cross_x)

    next_half = projection(1 - member, context, kv_weight[0])
    late_context, _ = lax.optimization_barrier((context, next_half))
    same_half = projection(member, late_context, kv_weight[0])
    same_half, qc_a, qc_b = lax.optimization_barrier((same_half, qc_a, qc_b))
    kv_blocks = [
        swapped(same_half, "tower"),
        moved_across(next_half, pair_x),
        moved_across(same_half, same_x),
        moved_across(next_half, cross_x),
        moved_across(same_half, next_row(False, 0)),
        moved_across(next_half, next_row(False, 1)),
    ]
    ctx_own = half_of(context, z)
    kv_blocks, late_own, ctx_rest = lax.optimization_barrier(
        (kv_blocks, ctx_own, half_of(context, 1 - z))
    )
    ctx_z = moved(ctx_rest, "seq", across_z())
    ctx_pair = moved(late_own, "seq", pair_x)

    span_a, span_b = qc_a[rows, :2].astype(jnp.int32), qc_b[rows, :2].astype(jnp.int32)
    first = jnp.where(member == 0, span_a, span_b)
    second = jnp.where(member == 0, span_b, span_a)
    base = position - member - 4 * side
    meta = jnp.concatenate([jnp.stack([member, base]), first, second, side[None]]).astype(jnp.int32)
    od_a, od_b, g_near, g_mid, g_far = attention(meta, qc_a, qc_b, kv_blocks)

    g_mid = moved_across(g_mid, same_x)
    g_near, ctx_pair, ctx_z = lax.optimization_barrier((g_near, ctx_pair, ctx_z))
    g_far = moved_across(g_far, next_row(True, 0))
    returned = total([swapped(g_near, "tower"), g_mid, g_far]).astype(BF16)
    late_z, _ = lax.optimization_barrier((ctx_z, returned))
    ctx_pair_z = moved(late_z, "seq", pair_x)
    returned_z = moved(returned, "seq", across_z())
    other_rows = moved(returned[rows:], "seq", pair_x)
    od_b, _ = lax.optimization_barrier((od_b, returned))
    od_b = moved(od_b, "seq", cross_x)
    other_rows, od_b = lax.optimization_barrier((other_rows, od_b))
    partial_ctx = context_partial(member, returned, other_rows, kv_weight[0])
    od_a, _ = lax.optimization_barrier((od_a, partial_ctx))
    od_a = moved(od_a, "seq", same_x)
    sum_parts = [partial_ctx[:, : width // 3], partial_ctx[:, width // 3 :]]
    sum_first = swapped(sum_parts[0], "mp")


    partial_w = weight_partial([ctx_own, ctx_z, ctx_pair, ctx_pair_z], [returned, returned_z])
    partial_w, sum_first, od_a = lax.optimization_barrier((partial_w, sum_first, od_a))
    late_half, _ = lax.optimization_barrier((sum_parts[1], sum_first))
    sum_second = swapped(late_half, "mp")
    plane = YS * XS
    groups = [[z_ * plane + i for i in range(plane)] for z_ in range(ZS)]
    parts = lax.all_to_all(
        partial_w.reshape(plane, -1, columns), "seq", 0, 0, axis_index_groups=groups
    )
    weight_grad = weight_total(parts)[None]

    context_grad = jnp.concatenate(
        [
            total([mine, other]).astype(BF16)
            for mine, other in zip(sum_parts, (sum_first, sum_second))
        ],
        axis=1,
    )
    attn_out = in_order(od_a[:, : columns // 2], od_b[:, : columns // 2])
    query_grad = in_order(od_a[:, columns // 2 :], od_b[:, columns // 2 :])
    return attn_out[None], query_grad[None], context_grad[None], weight_grad


def solution(mesh):
    return jax.shard_map(
        local,
        mesh=mesh,
        in_specs=(
            P("tower", "seq", "mp"),
            P("tower", "seq", None),
            P("tower", None, None, "mp"),
            P("tower", "seq", None),
            P("tower", "seq", "mp"),
        ),
        out_specs=(
            P("tower", "seq", "mp"),
            P("tower", "seq", "mp"),
            P("tower", "seq", None),
            P("tower", "seq", None, "mp"),
        ),
        check_vma=False,
    )
```
